512 devices in a mesh: step: 8 (over x, core), row: 64 (over z, y).
Axes of the slice: x: 4, y: 8, z: 8, core: 2. Of those that a mesh axis runs over, the one named last changes fastest.
Arguments:
- trajectory: float32 [8, 4, 256, 128], P('step', None, 'row')
- noise: float32 [8, 4, 256, 128], P('step', None, 'row'), may hold values from -6 to 6
- tsteps: int32 [8, 2], P('step'), may hold values from 847 to 900, as said below
- w_in: bfloat16 [3, 3, 320, 4], replicated, may hold values from -1 to 1
- w_one: bfloat16 [3, 3, 320, 320], replicated, may hold values from -0.109375 to 0.109375
- w_two: bfloat16 [3, 3, 320, 320], replicated, may hold values from -0.109375 to 0.109375
- w_out: bfloat16 [3, 3, 4, 320], replicated, may hold values from -0.109375 to 0.109375
- w_time1: bfloat16 [320, 1280], replicated, may hold values from -0.3125 to 0.3125
- w_time2: bfloat16 [1280, 1280], replicated, may hold values from -0.15625 to 0.15625
- w_tproj: bfloat16 [1280, 320], replicated, may hold values from -0.15625 to 0.15625
Outputs:
- advanced: float32 [8, 4, 256, 128], P('step', None, 'row')
- slot_error: float32 [8], P('step')
The draws below stay inside these ranges and needn't reach their ends.
Inputs may be any that keep to these rules, and one draw needn't show every extreme that they name: tsteps[0, 0] is 900; tsteps[i, 0] = 900 - 6 i - j with j of 0 to 5 for i > 0, and j = 5 for the last slot; tsteps[i, 1] = tsteps[i + 1, 0], and tsteps[i, 0] - 6 for the last slot.
All inputs are finite; a program needn't handle non-finite values.
Results may differ from the reference program's by a relative error of at most 0.0003.
Values may be sent and summed in bfloat16 or wider, within the bound.
A program may use at most 64 MiB of HBM per device.

```python
import math
import jax
import jax.numpy as jnp
from jax import lax

C = 320
TEMB = 1280
LATENT = 4
GROUPS = 32
ROW_W = 128
HEIGHT = 256
WINDOW = 8


def draw_trajectory(key, part):
    key = jax.random.fold_in(key, 11)
    place = jnp.arange(HEIGHT, dtype=jnp.float32) / max(HEIGHT - 1, 1)
    base = jax.random.normal(key, (WINDOW, LATENT, HEIGHT, ROW_W), jnp.float32)
    scale = 3.0 ** place
    return base * scale[None, None, :, None]


def draw_tsteps(key, part):
    key = jax.random.fold_in(key, 12)
    jitter = jax.random.randint(key, (WINDOW,), 0, 6, dtype=jnp.int32)
    place = jnp.arange(WINDOW, dtype=jnp.int32)
    jitter = jnp.where(place == 0, 0, jitter)
    jitter = jnp.where(place == WINDOW - 1, 5, jitter)
    current = 900 - 6 * place - jitter
    following = jnp.concatenate([current[1:], current[-1:] - 6])
    return jnp.stack([current, following], axis=1).astype(jnp.int32)


def steps_of(key, shape, cuts, low, top_value):
    loudness = 1.0
    for dim, parts in cuts:
        steps = jax.random.uniform(jax.random.fold_in(jax.random.fold_in(key, 6), dim), (parts,), jnp.float32, low / len(cuts), top_value / len(cuts))
        loudness = loudness * jnp.repeat(jnp.exp(steps), shape[dim] // parts).reshape((-1,) + (1,) * (len(shape) - 1 - dim))
    return loudness


def scatter_about(rng, extent, deviation, reach, pieces=(), kind=jnp.bfloat16):
    drawn = deviation * jax.random.normal(rng, extent, jnp.float32)
    if pieces:
        drawn = drawn * steps_of(rng, extent, pieces, -0.22, 0.18)
    return jnp.clip(drawn, -reach, reach).astype(kind)


def setup_inputs(seed: int = 0) -> dict:
    splits = jax.random.split(jax.random.key(seed), 11)
    return {
        "trajectory": draw_trajectory(jax.random.fold_in(splits[10], 71), 0),
        "noise": scatter_about(splits[1], (WINDOW, LATENT, HEIGHT, ROW_W), 1.0, 6.0, ((0, 8), (2, 64)), jnp.float32),
        "tsteps": draw_tsteps(jax.random.fold_in(splits[10], 71), 0),
        "w_in": scatter_about(splits[3], (3, 3, C, LATENT), (9 * LATENT) ** -0.5, 1.0),
        "w_one": scatter_about(splits[4], (3, 3, C, C), (9 * C) ** -0.5, 0.109375),
        "w_two": scatter_about(splits[5], (3, 3, C, C), (9 * C) ** -0.5, 0.109375),
        "w_out": scatter_about(splits[6], (3, 3, LATENT, C), (9 * C) ** -0.5, 0.109375),
        "w_time1": scatter_about(splits[7], (C, TEMB), C ** -0.5, 0.3125),
        "w_time2": scatter_about(splits[8], (TEMB, TEMB), TEMB ** -0.5, 0.15625),
        "w_tproj": scatter_about(splits[9], (TEMB, C), TEMB ** -0.5, 0.15625),
    }


noise_share = 0.5
norm_eps = 1e-05

def alpha_bar(level):
    angle = (level.astype(jnp.float32) / 1000.0 + 0.008) / 1.008 * (math.pi / 2)
    return jnp.cos(angle) ** 2

def conv_taps(padded, weight):
    channels, rows_in, width = padded.shape
    rows = rows_in - 2
    wide = jnp.pad(padded, ((0, 0), (0, 0), (1, 1)))
    total = jnp.zeros((weight.shape[2], rows * width), jnp.float32)
    for row_off in range(3):
        for col_off in range(3):
            window = wide[:, row_off:row_off + rows, col_off:col_off + width].reshape(channels, rows * width)
            total = total + jnp.dot(weight[row_off, col_off], window, preferred_element_type=jnp.float32)
    return total.reshape(weight.shape[2], rows, width)

def full_conv(feature, weight):
    return conv_taps(jnp.pad(feature, ((0, 0), (1, 1), (0, 0))), weight)

def normalize(feature):
    channels, rows, width = feature.shape
    grouped = feature.reshape(GROUPS, channels // GROUPS, rows, width)
    mean = lax.optimization_barrier(jnp.mean(grouped, axis=(1, 2, 3), keepdims=True))
    square = lax.optimization_barrier(jnp.mean(grouped * grouped, axis=(1, 2, 3), keepdims=True))
    return ((grouped - mean) * lax.rsqrt(square - mean * mean + norm_eps)).reshape(channels, rows, width)

def time_vector(level, w_time1, w_time2, w_tproj):
    half = w_time1.shape[0] // 2
    freq = jnp.exp(-math.log(10000.0) * jnp.arange(half, dtype=jnp.float32) / half)
    angle = level.astype(jnp.float32) * freq
    embed = jnp.concatenate([jnp.cos(angle), jnp.sin(angle)]).astype(jnp.bfloat16)
    hidden = jax.nn.silu(jnp.dot(embed, w_time1, preferred_element_type=jnp.float32)).astype(jnp.bfloat16)
    second = jax.nn.silu(jnp.dot(hidden, w_time2, preferred_element_type=jnp.float32)).astype(jnp.bfloat16)
    return jnp.dot(second, w_tproj, preferred_element_type=jnp.float32)

def coefficients(level, level_next):
    now = alpha_bar(level)
    after = alpha_bar(level_next)
    sigma = noise_share * jnp.sqrt((1.0 - after) / (1.0 - now) * (1.0 - now / after))
    keep_x = jnp.sqrt(after / now)
    keep_e = jnp.sqrt(1.0 - after - sigma * sigma) - jnp.sqrt(after) * jnp.sqrt(1.0 - now) / jnp.sqrt(now)
    return (keep_x, keep_e, sigma)

def slot_drift(state, fresh, level, level_next, w_in, w_one, w_two, w_out, w_time1, w_time2, w_tproj):
    tvec = time_vector(level, w_time1, w_time2, w_tproj)
    first = full_conv(state.astype(jnp.bfloat16), w_in)
    act = jax.nn.silu(normalize(first)).astype(jnp.bfloat16)
    second = full_conv(act, w_one) + tvec[:, None, None]
    act = jax.nn.silu(normalize(second)).astype(jnp.bfloat16)
    joined = first + full_conv(act, w_two)
    act = jax.nn.silu(normalize(joined)).astype(jnp.bfloat16)
    predicted = full_conv(act, w_out)
    keep_x, keep_e, sigma = coefficients(level, level_next)
    return keep_x * state + keep_e * predicted + sigma * fresh - state

def reference(trajectory, noise, tsteps, w_in, w_one, w_two, w_out, w_time1, w_time2, w_tproj):

    def one(item):
        return slot_drift(item[0], item[1], item[2], item[3], w_in, w_one, w_two, w_out, w_time1, w_time2, w_tproj)
    drifts = lax.map(one, (trajectory, noise, tsteps[:, 0], tsteps[:, 1]))
    terms = drifts.at[0].add(trajectory[0])
    advanced = jnp.cumsum(terms, axis=0)
    earlier = jnp.concatenate([jnp.zeros_like(terms[:1]), advanced[:-1]], axis=0).at[0].set(trajectory[0])
    slot_error = lax.optimization_barrier(jnp.mean((earlier - trajectory) ** 2, axis=(1, 2, 3)))
    return (advanced, slot_error)
```

```python
import functools
import math

import jax
import jax.numpy as jnp
from jax import lax
from jax.experimental import pallas as pl
from jax.experimental.pallas import tpu as pltpu
from jax.sharding import PartitionSpec as P

MESH = pl.DeviceIdType.MESH
F32 = jnp.float32
BF16 = jnp.bfloat16
LATENT = 4
GROUPS = 32
LANES = 128
ROWS = 4
NORM_EPS = 1e-05
NOISE_SHARE = 0.5


def dot(a, b):
    return jnp.dot(a, b, preferred_element_type=F32)


def offsets(nz, ny):
    hops = lambda d, n: min(d, n - d)
    every = [(dz, dy) for dz in range(nz) for dy in range(ny) if (dz, dy) != (0, 0)]
    return sorted(every, key=lambda o: -(hops(o[0], nz) + hops(o[1], ny)))


def silu(x):
    return x / (1.0 + jnp.exp(-x))


def shifted(x, col):
    if col == 1:
        return x
    lane = lax.broadcasted_iota(jnp.int32, x.shape, x.ndim - 1)
    if col == 0:
        return jnp.where(lane == 0, 0.0, pltpu.roll(x, 1, axis=x.ndim - 1))
    return jnp.where(lane == LANES - 1, 0.0, pltpu.roll(x, LANES - 1, axis=x.ndim - 1))


def kernel(
    nz, ny, nsteps, channels, temb, height,
    traj_h, noise_h, ts_h, w_in_h, w_one_h, w_two_h, w_out_h, wt1_h, wt2_h, wtp_h,
    adv_ref, err_ref,
    traj, noise, ts, w_in, w_one, w_two, w_out, wt1, wt2, wtp,
    win_f, win_m, wone_m, wtwo_m, wout_f,
    xbuf, xcol, h0, h1, rr, acts, vt, mcol, scol, tcol,
    msg, sums, terms, tbuf,
    load_sem, x_send, x_recv, h_send, h_recv, ar_send, ar_recv, t_send, t_recv,
):
    nrow = nz * ny
    row = lax.axis_index("row")
    step = lax.axis_index("step")
    mz, my = row // ny, lax.rem(row, ny)
    peers = [
        lax.rem(mz + dz, nz) * ny + lax.rem(my + dy, ny) for dz, dy in offsets(nz, ny)
    ]
    others = [lax.rem(step + d, nsteps) for d in range(1, nsteps)]
    below = lax.rem(row + 1, nrow)
    above = lax.rem(row + nrow - 1, nrow)
    per_group = channels // GROUPS

    barrier = pltpu.get_barrier_semaphore()
    for p in peers:
        pl.semaphore_signal(barrier, inc=1, device_id={"row": p}, device_id_type=MESH)
    for s in others:
        pl.semaphore_signal(barrier, inc=1, device_id={"step": s}, device_id_type=MESH)

    loads = [
        (traj_h, traj), (noise_h, noise), (ts_h, ts), (w_in_h, w_in), (w_one_h, w_one),
        (wt1_h, wt1), (wt2_h, wt2), (wtp_h, wtp), (w_two_h, w_two), (w_out_h, w_out),
    ]
    copies = [
        pltpu.make_async_copy(src, dst, load_sem.at[i]) for i, (src, dst) in enumerate(loads)
    ]
    for c in copies:
        c.start()
    (c_traj, c_noise, c_ts, c_win, c_wone, c_wt1, c_wt2, c_wtp, c_wtwo, c_wout) = copies

    c_traj.wait()
    for r in range(ROWS):
        xbuf[2 + r] = traj[0, :, r, :]

    xcol[...] = jnp.zeros_like(xcol)
    win_f[...] = jnp.zeros_like(win_f)
    c_win.wait()
    for p in range(3):
        for q in range(3):
            tap = 4 * (3 * p + q)
            win_f[tap : tap + 4, :channels] = w_in[p, q].astype(F32)
    win_m[...] = jnp.transpose(win_f[...])[:channels].astype(BF16)

    pl.semaphore_wait(barrier, nrow - 1 + nsteps - 1)

    up = pltpu.make_async_remote_copy(
        xbuf.at[pl.ds(2, 2)], xbuf.at[pl.ds(6, 2)], x_send.at[0], x_recv.at[0],
        device_id={"row": above}, device_id_type=MESH,
    )
    down = pltpu.make_async_remote_copy(
        xbuf.at[pl.ds(4, 2)], xbuf.at[pl.ds(0, 2)], x_send.at[1], x_recv.at[1],
        device_id={"row": below}, device_id_type=MESH,
    )
    up.start()
    down.start()

    def merge(weights, merged):
        for q in range(3):
            merged[q] = jnp.concatenate([weights[p, q] for p in range(3)], axis=1)

    c_wone.wait()
    merge(w_one, wone_m)

    is_top = row == 0
    is_bottom = row == nrow - 1

    def send_sums(k, line):
        msg[k] = line
        sums[k, pl.ds(row, 1), :] = line
        for p in peers:
            pltpu.make_async_remote_copy(
                msg.at[k], sums.at[k, pl.ds(row, 1), :], ar_send.at[k], ar_recv.at[k],
                device_id={"row": p}, device_id_type=MESH,
            ).start()

    def others_of(k):
        return sums.at[k, pl.ds(0, nrow - 1), :]

    def total_sums(k):
        part = others_of(k)
        pltpu.make_async_copy(part, part, ar_recv.at[k]).wait()
        return jnp.sum(sums[k], axis=0, keepdims=True)

    group_of = lax.broadcasted_iota(jnp.int32, (GROUPS, channels), 0) * per_group
    channel = lax.broadcasted_iota(jnp.int32, (GROUPS, channels), 1)
    members = jnp.where(
        (channel >= group_of) & (channel < group_of + per_group), 1.0, 0.0
    ).astype(BF16)

    def group_line(rows):
        total = functools.reduce(lambda a, b: a + b, rows)
        square = functools.reduce(lambda a, b: a + b, [v * v for v in rows])
        both = jnp.concatenate([total, square], axis=1)
        high = both.astype(BF16)
        rest = both - high.astype(F32)
        mid = rest.astype(BF16)
        low = (rest - mid.astype(F32)).astype(BF16)
        grouped = dot(members, high) + dot(members, mid) + dot(members, low)
        stacked = jnp.concatenate(
            [grouped[:, :LANES], grouped[:, LANES:], jnp.zeros((64, LANES), F32)], axis=0
        )
        return jnp.sum(jnp.transpose(stacked), axis=0, keepdims=True)

    count = per_group * height * LANES

    def norm_columns(k):
        total = total_sums(k) * (1.0 / count)
        lane = lax.broadcasted_iota(jnp.int32, total.shape, 1)
        square = pltpu.roll(total, LANES - GROUPS, axis=1)
        variance = jnp.where(lane < GROUPS, square - total * total, 1.0)
        scale = lax.rsqrt(variance + NORM_EPS)
        line = jnp.where(lane < GROUPS, total, pltpu.roll(scale, GROUPS, axis=1))
        vt[...] = jnp.transpose(jnp.broadcast_to(line, (LANES, LANES)))
        sub = lax.broadcasted_iota(jnp.int32, (8, LANES), 0)
        for first, target in ((0, mcol), (GROUPS, scol)):
            for j in range(channels // 8):
                low, high = 8 * j // per_group, (8 * j + 7) // per_group
                value = jnp.broadcast_to(vt[first + low : first + low + 1, :], (8, LANES))
                if high != low:
                    other = jnp.broadcast_to(vt[first + high : first + high + 1, :], (8, LANES))
                    value = jnp.where(sub < high * per_group - 8 * j, value, other)
                target[8 * j : 8 * j + 8, :] = value

    def activate(source, r):
        act = silu((source[r] - mcol[...]) * scol[...])
        if r == 0:
            act = jnp.where(is_top, 0.0, act)
        if r == ROWS + 1:
            act = jnp.where(is_bottom, 0.0, act)
        return act.astype(BF16)

    def place(r, act):
        for p in range(3):
            if 0 <= r - p < ROWS:
                acts[p * channels : (p + 1) * channels, (r - p) * LANES : (r - p + 1) * LANES] = act

    def conv(merged, source, finish):
        for r in range(ROWS + 2):
            place(r, activate(source, r))
        for half in range(ROWS // 2):
            x = acts[:, half * 2 * LANES : (half + 1) * 2 * LANES]
            y = [dot(merged[q], x) for q in range(3)]
            for i in range(2):
                cut = slice(i * LANES, (i + 1) * LANES)
                finish(2 * half + i, sum(shifted(y[q][:, cut], q) for q in range(3)))

    def halo_copies(buf, k):
        return [
            pltpu.make_async_remote_copy(
                buf.at[1], buf.at[ROWS + 1], h_send.at[k, 0], h_recv.at[k, 0],
                device_id={"row": above}, device_id_type=MESH,
            ),
            pltpu.make_async_remote_copy(
                buf.at[ROWS], buf.at[0], h_send.at[k, 1], h_recv.at[k, 1],
                device_id={"row": below}, device_id_type=MESH,
            ),
        ]

    up.wait_recv()
    down.wait_recv()
    for r in range(ROWS + 4):
        x = xbuf[r]
        if r < 2:
            x = jnp.where(is_top, 0.0, x)
        if r >= ROWS + 2:
            x = jnp.where(is_bottom, 0.0, x)
        for q in range(3):
            moved = shifted(x, q)
            for p in range(3):
                if 0 <= r - p < ROWS + 2:
                    tap = 4 * (3 * p + q)
                    xcol[tap : tap + 4, (r - p) * LANES : (r - p + 1) * LANES] = moved
    first = dot(win_m[:, :48], xcol[...].astype(BF16))
    for r in range(ROWS + 2):
        h0[r] = first[:, r * LANES : (r + 1) * LANES]
    send_sums(0, group_line([h0[r] for r in range(1, ROWS + 1)]))

    c_ts.wait()
    times = ts[...].astype(F32)
    level = jnp.broadcast_to(times[:, 0:1], (1, LANES))
    level_next = jnp.broadcast_to(times[:, 1:2], (1, LANES))
    c_wt1.wait()
    half = channels // 2
    lane = lax.broadcasted_iota(jnp.int32, (LANES, channels), 1)
    place_of = jnp.where(lane < half, lane, lane - half).astype(F32)
    freq = jnp.exp(-math.log(10000.0) * place_of / half)
    angle = jnp.broadcast_to(times[:, 0:1], (LANES, channels)) * freq
    embed = jnp.where(lane < half, jnp.cos(angle), jnp.sin(angle)).astype(BF16)
    hidden = silu(dot(embed, wt1[...])).astype(BF16)
    c_wt2.wait()
    second = silu(dot(hidden, wt2[...])).astype(BF16)
    c_wtp.wait()
    tcol[...] = lax.dot_general(
        wtp[...], second, (((1,), (1,)), ((), ())), preferred_element_type=F32
    )

    c_wtwo.wait()
    merge(w_two, wtwo_m)
    c_wout.wait()
    wout_f[...] = jnp.zeros_like(wout_f)
    for p in range(3):
        for q in range(3):
            tap = 8 * (3 * p + q)
            wout_f[tap : tap + 4, :] = w_out[p, q].astype(F32)

    def alpha_bar(t):
        return jnp.cos((t / 1000.0 + 0.008) / 1.008 * (math.pi / 2)) ** 2

    now, after = alpha_bar(level), alpha_bar(level_next)
    sigma = NOISE_SHARE * jnp.sqrt((1.0 - after) / (1.0 - now) * (1.0 - now / after))
    keep_x = jnp.sqrt(after / now)
    keep_e = jnp.sqrt(1.0 - after - sigma * sigma) - jnp.sqrt(after) * jnp.sqrt(
        1.0 - now
    ) / jnp.sqrt(now)

    norm_columns(0)

    def finish_one(r, value):
        h1[1 + r] = value + tcol[...]

    conv(wone_m, h0, finish_one)
    halo1 = halo_copies(h1, 0)
    for c in halo1:
        c.start()
    send_sums(1, group_line([h1[r] for r in range(1, ROWS + 1)]))

    norm_columns(1)
    for c in halo1:
        c.wait_recv()

    def finish_two(r, value):
        rr[1 + r] = value + h0[1 + r]

    conv(wtwo_m, h1, finish_two)
    halo2 = halo_copies(rr, 1)
    for c in halo2:
        c.start()
    send_sums(2, group_line([rr[r] for r in range(1, ROWS + 1)]))

    c_noise.wait()
    norm_columns(2)
    for c in halo2:
        c.wait_recv()
    a3 = jnp.concatenate([activate(rr, r) for r in range(ROWS + 2)], axis=1)
    y = dot(wout_f[...].astype(BF16), a3)
    is_first = step == 0
    for r in range(ROWS):
        eps = jnp.zeros((8, LANES), F32)
        for q in range(3):
            column = jnp.zeros((8, LANES), F32)
            for p in range(3):
                tap = 8 * (3 * p + q)
                column += y[tap : tap + 8, (r + p) * LANES : (r + p + 1) * LANES]
            eps += shifted(column, q)
        x = traj[0, :, r, :]
        term = keep_x * x + keep_e * eps[:LATENT] + sigma * noise[0, :, r, :] - x
        term = term + jnp.where(is_first, x, 0.0)
        tbuf[r] = term
        terms[step, r] = term

    for s in others:
        pltpu.make_async_remote_copy(
            tbuf, terms.at[step], t_send, t_recv, device_id={"step": s}, device_id_type=MESH,
        ).start()
    came = terms.at[pl.ds(0, nsteps - 1)]
    pltpu.make_async_copy(came, came, t_recv).wait()
    error = jnp.zeros((LATENT, LANES), F32)
    for r in range(ROWS):
        earlier = jnp.zeros((LATENT, LANES), F32)
        for s in range(nsteps - 1):
            earlier = earlier + jnp.where(s < step, terms[s, r], 0.0)
        adv_ref[0, :, r, :] = earlier + tbuf[r]
        x = traj[0, :, r, :]
        gap = jnp.where(is_first, 0.0, earlier - x)
        error = error + gap * gap
    send_sums(3, jnp.sum(error, axis=0, keepdims=True))
    err_ref[0] = jnp.sum(total_sums(3)) * (1.0 / (LATENT * height * LANES))

    up.wait_send()
    down.wait_send()
    for c in halo1 + halo2:
        c.wait_send()
    for k in range(4):
        part = others_of(k)
        pltpu.make_async_copy(part, part, ar_send.at[k]).wait()
    pltpu.make_async_copy(came, came, t_send).wait()


def shards(nz, ny, nsteps, trajectory, noise, tsteps, w_in, w_one, w_two, w_out, wt1, wt2, wtp):
    w_in = jnp.transpose(w_in, (0, 1, 3, 2))
    wtp = jnp.transpose(wtp)
    args = (trajectory, noise, tsteps, w_in, w_one, w_two, w_out, wt1, wt2, wtp)
    channels, temb = wt1.shape
    nrow = nz * ny
    height = trajectory.shape[2] * nrow
    vmem = lambda shape, dtype: pltpu.VMEM(shape, dtype)
    scratch = [vmem(a.shape, a.dtype) for a in args] + [
        vmem((LANES, -(-channels // LANES) * LANES), F32),
        vmem((channels, LANES), BF16),
        vmem((3, channels, 3 * channels), BF16),
        vmem((3, channels, 3 * channels), BF16),
        vmem((80, channels), F32),
        vmem((ROWS + 4, LATENT, LANES), F32),
        vmem((48, (ROWS + 2) * LANES), F32),
        vmem((ROWS + 2, channels, LANES), F32),
        vmem((ROWS + 2, channels, LANES), F32),
        vmem((ROWS + 2, channels, LANES), F32),
        vmem((3 * channels, ROWS * LANES), BF16),
        vmem((LANES, LANES), F32),
        vmem((channels, LANES), F32),
        vmem((channels, LANES), F32),
        vmem((channels, LANES), F32),
        vmem((4, 1, LANES), F32),
        vmem((4, nrow, LANES), F32),
        vmem((nsteps, ROWS, LATENT, LANES), F32),
        vmem((ROWS, LATENT, LANES), F32),
        pltpu.SemaphoreType.DMA((len(args),)),
        pltpu.SemaphoreType.DMA((2,)),
        pltpu.SemaphoreType.DMA((2,)),
        pltpu.SemaphoreType.DMA((2, 2)),
        pltpu.SemaphoreType.DMA((2, 2)),
        pltpu.SemaphoreType.DMA((4,)),
        pltpu.SemaphoreType.DMA((4,)),
        pltpu.SemaphoreType.DMA,
        pltpu.SemaphoreType.DMA,
    ]
    return pl.pallas_call(
        functools.partial(kernel, nz, ny, nsteps, channels, temb, height),
        out_shape=(
            jax.ShapeDtypeStruct(trajectory.shape, F32),
            jax.ShapeDtypeStruct((1,), F32),
        ),
        in_specs=[pl.BlockSpec(memory_space=pltpu.HBM)] * len(args),
        out_specs=(
            pl.BlockSpec(memory_space=pltpu.VMEM),
            pl.BlockSpec(memory_space=pltpu.SMEM),
        ),
        scratch_shapes=scratch,
        compiler_params=pltpu.CompilerParams(
            collective_id=0, has_side_effects=True, vmem_limit_bytes=56 * 1024 * 1024
        ),
    )(*args)


def solution(mesh):
    nsteps, nrow = mesh.shape["step"], mesh.shape["row"]
    ny = 8 if nrow % 8 == 0 else 2
    place = P("step", None, "row", None)
    return jax.shard_map(
        functools.partial(shards, nrow // ny, ny, nsteps),
        mesh=mesh,
        in_specs=(place, place, P("step", None)) + (P(),) * 7,
        out_specs=(place, P("step")),
        check_vma=False,
    )
```

```python
import functools
import math

import jax
import jax.numpy as jnp
from jax import lax
from jax.experimental import pallas as pl
from jax.experimental.pallas import tpu as pltpu
from jax.sharding import PartitionSpec as P

MESH = pl.DeviceIdType.MESH
F32 = jnp.float32
BF16 = jnp.bfloat16
LATENT = 4
GROUPS = 32
LANES = 128
ROWS = 4
NORM_EPS = 1e-05
NOISE_SHARE = 0.5


def dot(a, b):
    return jnp.dot(a, b, preferred_element_type=F32)


def offsets(nz, ny):
    hops = lambda d, n: min(d, n - d)
    every = [(dz, dy) for dz in range(nz) for dy in range(ny) if (dz, dy) != (0, 0)]
    return sorted(every, key=lambda o: -(hops(o[0], nz) + hops(o[1], ny)))


def silu(x):
    half = 0.5 * x
    return half + half * jnp.tanh(half)


def shifted(x, col):
    if col == 1:
        return x
    lane = lax.broadcasted_iota(jnp.int32, x.shape, x.ndim - 1)
    if col == 0:
        return jnp.where(lane == 0, 0.0, pltpu.roll(x, 1, axis=x.ndim - 1))
    return jnp.where(lane == LANES - 1, 0.0, pltpu.roll(x, LANES - 1, axis=x.ndim - 1))


def kernel(
    nz, ny, nsteps, channels, temb, height,
    traj_h, noise_h, ts_h, w_in_h, w_one_h, w_two_h, w_out_h, wt1_h, wt2_h, wtp_h,
    adv_ref, err_ref,
    traj, noise, ts, w_in, w_one, w_two, w_out, wt1, wt2, wtp,
    win_f, win_m, wone_m, wtwo_m, wout_f,
    xbuf, xcol, h0, h1, rr, acts, vt, mcol, scol, tcol,
    msg, sums, terms, tbuf,
    load_sem, x_send, x_recv, h_send, h_recv, ar_send, ar_recv, t_send, t_recv, line_sem, adv, err, out_sem,
):
    nrow = nz * ny
    row = lax.axis_index("row")
    step = lax.axis_index("step")
    mz, my = row // ny, lax.rem(row, ny)
    peers = [
        lax.rem(mz + dz, nz) * ny + lax.rem(my + dy, ny) for dz, dy in offsets(nz, ny)
    ]
    others = [lax.rem(step + d, nsteps) for d in range(1, nsteps)]
    below = lax.rem(row + 1, nrow)
    above = lax.rem(row + nrow - 1, nrow)
    per_group = channels // GROUPS

    column = [lax.rem(mz + d, nz) * ny + my for d in range(1, nz)]
    line = [mz * ny + lax.rem(my + d, ny) for d in range(1, ny)]
    barrier = pltpu.get_barrier_semaphore()
    for p in column + line + [above, below]:
        pl.semaphore_signal(barrier, inc=1, device_id={"row": p}, device_id_type=MESH)
    for s in others:
        pl.semaphore_signal(barrier, inc=1, device_id={"step": s}, device_id_type=MESH)

    loads = [
        (traj_h, traj), (noise_h, noise), (ts_h, ts), (w_in_h, w_in), (w_one_h, w_one),
        (wt1_h, wt1), (wt2_h, wt2), (wtp_h, wtp), (w_two_h, w_two), (w_out_h, w_out),
    ]
    copies = [
        pltpu.make_async_copy(src, dst, load_sem.at[i]) for i, (src, dst) in enumerate(loads)
    ]
    for c in copies:
        c.start()
    (c_traj, c_noise, c_ts, c_win, c_wone, c_wt1, c_wt2, c_wtp, c_wtwo, c_wout) = copies

    c_traj.wait()
    for r in range(ROWS):
        xbuf[2 + r] = traj[0, :, r, :]

    xcol[...] = jnp.zeros_like(xcol)
    win_f[...] = jnp.zeros_like(win_f)
    c_win.wait()
    for p in range(3):
        for q in range(3):
            tap = 4 * (3 * p + q)
            win_f[tap : tap + 4, :channels] = w_in[p, q].astype(F32)
    win_m[...] = jnp.transpose(win_f[...])[:channels].astype(BF16)

    pl.semaphore_wait(barrier, nz - 1 + ny - 1 + 2 + nsteps - 1)

    up = pltpu.make_async_remote_copy(
        xbuf.at[pl.ds(2, 2)], xbuf.at[pl.ds(6, 2)], x_send.at[0], x_recv.at[0],
        device_id={"row": above}, device_id_type=MESH,
    )
    down = pltpu.make_async_remote_copy(
        xbuf.at[pl.ds(4, 2)], xbuf.at[pl.ds(0, 2)], x_send.at[1], x_recv.at[1],
        device_id={"row": below}, device_id_type=MESH,
    )
    up.start()
    down.start()
    for p in column:
        pl.semaphore_signal(line_sem, inc=1, device_id={"row": p}, device_id_type=MESH)

    def merge(weights, merged):
        for q in range(3):
            merged[q] = jnp.concatenate([weights[p, q] for p in range(3)], axis=1)

    c_wone.wait()
    merge(w_one, wone_m)

    is_top = row == 0
    is_bottom = row == nrow - 1

    def send_sums(k, line):
        msg[k] = line
        sums[k, pl.ds(row, 1), :] = line
        for p in peers:
            pltpu.make_async_remote_copy(
                msg.at[k], sums.at[k, pl.ds(row, 1), :], ar_send.at[k], ar_recv.at[k],
                device_id={"row": p}, device_id_type=MESH,
            ).start()

    def others_of(k):
        return sums.at[k, pl.ds(0, nrow - 1), :]

    def total_sums(k):
        part = others_of(k)
        pltpu.make_async_copy(part, part, ar_recv.at[k]).wait()
        return jnp.sum(sums[k], axis=0, keepdims=True)

    group_of = lax.broadcasted_iota(jnp.int32, (GROUPS, channels), 0) * per_group
    channel = lax.broadcasted_iota(jnp.int32, (GROUPS, channels), 1)
    members = jnp.where(
        (channel >= group_of) & (channel < group_of + per_group), 1.0, 0.0
    ).astype(BF16)

    def group_line(rows):
        total = functools.reduce(lambda a, b: a + b, rows)
        square = functools.reduce(lambda a, b: a + b, [v * v for v in rows])
        both = jnp.concatenate([total, square], axis=1)
        high = both.astype(BF16)
        rest = both - high.astype(F32)
        mid = rest.astype(BF16)
        low = (rest - mid.astype(F32)).astype(BF16)
        grouped = dot(members, high) + dot(members, mid) + dot(members, low)
        stacked = jnp.concatenate(
            [grouped[:, :LANES], grouped[:, LANES:], jnp.zeros((64, LANES), F32)], axis=0
        )
        return jnp.sum(jnp.transpose(stacked), axis=0, keepdims=True)

    count = per_group * height * LANES

    def norm_columns(k):
        total = total_sums(k) * (1.0 / count)
        lane = lax.broadcasted_iota(jnp.int32, total.shape, 1)
        square = pltpu.roll(total, LANES - GROUPS, axis=1)
        variance = jnp.where(lane < GROUPS, square - total * total, 1.0)
        scale = lax.rsqrt(variance + NORM_EPS)
        line = jnp.where(lane < GROUPS, total, pltpu.roll(scale, GROUPS, axis=1))
        vt[...] = jnp.transpose(jnp.broadcast_to(line, (LANES, LANES)))
        sub = lax.broadcasted_iota(jnp.int32, (8, LANES), 0)
        for first, target in ((0, mcol), (GROUPS, scol)):
            for j in range(channels // 8):
                low, high = 8 * j // per_group, (8 * j + 7) // per_group
                value = jnp.broadcast_to(vt[first + low : first + low + 1, :], (8, LANES))
                if high != low:
                    other = jnp.broadcast_to(vt[first + high : first + high + 1, :], (8, LANES))
                    value = jnp.where(sub < high * per_group - 8 * j, value, other)
                target[8 * j : 8 * j + 8, :] = value

    def activate(source, r):
        act = silu((source[r] - mcol[...]) * scol[...])
        if r == 0:
            act = jnp.where(is_top, 0.0, act)
        if r == ROWS + 1:
            act = jnp.where(is_bottom, 0.0, act)
        return act.astype(BF16)

    def place(r, act):
        for p in range(3):
            if 0 <= r - p < ROWS:
                acts[p * channels : (p + 1) * channels, (r - p) * LANES : (r - p + 1) * LANES] = act

    def conv(merged, source, finish):
        for r in range(ROWS + 2):
            place(r, activate(source, r))
        for half in range(ROWS // 2):
            x = acts[:, half * 2 * LANES : (half + 1) * 2 * LANES]
            y = [dot(merged[q], x) for q in range(3)]
            for i in range(2):
                cut = slice(i * LANES, (i + 1) * LANES)
                finish(2 * half + i, sum(shifted(y[q][:, cut], q) for q in range(3)))

    def halo_copies(buf, k):
        return [
            pltpu.make_async_remote_copy(
                buf.at[1], buf.at[ROWS + 1], h_send.at[k, 0], h_recv.at[k, 0],
                device_id={"row": above}, device_id_type=MESH,
            ),
            pltpu.make_async_remote_copy(
                buf.at[ROWS], buf.at[0], h_send.at[k, 1], h_recv.at[k, 1],
                device_id={"row": below}, device_id_type=MESH,
            ),
        ]

    up.wait_recv()
    down.wait_recv()
    for r in range(ROWS + 4):
        x = xbuf[r]
        if r < 2:
            x = jnp.where(is_top, 0.0, x)
        if r >= ROWS + 2:
            x = jnp.where(is_bottom, 0.0, x)
        for q in range(3):
            moved = shifted(x, q)
            for p in range(3):
                if 0 <= r - p < ROWS + 2:
                    tap = 4 * (3 * p + q)
                    xcol[tap : tap + 4, (r - p) * LANES : (r - p + 1) * LANES] = moved
    first = dot(win_m[:, :48], xcol[...].astype(BF16))
    for r in range(ROWS + 2):
        h0[r] = first[:, r * LANES : (r + 1) * LANES]
    pl.semaphore_wait(line_sem, nz - 1)
    send_sums(0, group_line([h0[r] for r in range(1, ROWS + 1)]))

    c_ts.wait()
    times = ts[...].astype(F32)
    level = jnp.broadcast_to(times[:, 0:1], (1, LANES))
    level_next = jnp.broadcast_to(times[:, 1:2], (1, LANES))
    c_wt1.wait()
    half = channels // 2
    lane = lax.broadcasted_iota(jnp.int32, (LANES, channels), 1)
    place_of = jnp.where(lane < half, lane, lane - half).astype(F32)
    freq = jnp.exp(-math.log(10000.0) * place_of / half)
    angle = jnp.broadcast_to(times[:, 0:1], (LANES, channels)) * freq
    embed = jnp.where(lane < half, jnp.cos(angle), jnp.sin(angle)).astype(BF16)
    hidden = silu(dot(embed, wt1[...])).astype(BF16)
    c_wt2.wait()
    second = silu(dot(hidden, wt2[...])).astype(BF16)
    c_wtp.wait()
    tcol[...] = lax.dot_general(
        wtp[...], second, (((1,), (1,)), ((), ())), preferred_element_type=F32
    )

    c_wtwo.wait()
    merge(w_two, wtwo_m)
    c_wout.wait()
    wout_f[...] = jnp.zeros_like(wout_f)
    for p in range(3):
        for q in range(3):
            tap = 8 * (3 * p + q)
            wout_f[tap : tap + 4, :] = w_out[p, q].astype(F32)

    def alpha_bar(t):
        return jnp.cos((t / 1000.0 + 0.008) / 1.008 * (math.pi / 2)) ** 2

    now, after = alpha_bar(level), alpha_bar(level_next)
    sigma = NOISE_SHARE * jnp.sqrt((1.0 - after) / (1.0 - now) * (1.0 - now / after))
    keep_x = jnp.sqrt(after / now)
    keep_e = jnp.sqrt(1.0 - after - sigma * sigma) - jnp.sqrt(after) * jnp.sqrt(
        1.0 - now
    ) / jnp.sqrt(now)

    norm_columns(0)

    def finish_one(r, value):
        h1[1 + r] = value + tcol[...]

    conv(wone_m, h0, finish_one)
    halo1 = halo_copies(h1, 0)
    send_sums(1, group_line([h1[r] for r in range(1, ROWS + 1)]))
    for c in halo1:
        c.start()

    norm_columns(1)
    for c in halo1:
        c.wait_recv()

    def finish_two(r, value):
        rr[1 + r] = value + h0[1 + r]

    conv(wtwo_m, h1, finish_two)
    halo2 = halo_copies(rr, 1)
    send_sums(2, group_line([rr[r] for r in range(1, ROWS + 1)]))
    for c in halo2:
        c.start()

    c_noise.wait()
    norm_columns(2)
    for c in halo2:
        c.wait_recv()
    a3 = jnp.concatenate([activate(rr, r) for r in range(ROWS + 2)], axis=1)
    y = dot(wout_f[...].astype(BF16), a3)
    is_first = step == 0
    for r in range(ROWS):
        eps = jnp.zeros((8, LANES), F32)
        for q in range(3):
            column = jnp.zeros((8, LANES), F32)
            for p in range(3):
                tap = 8 * (3 * p + q)
                column += y[tap : tap + 8, (r + p) * LANES : (r + p + 1) * LANES]
            eps += shifted(column, q)
        x = traj[0, :, r, :]
        term = keep_x * x + keep_e * eps[:LATENT] + sigma * noise[0, :, r, :] - x
        term = term + jnp.where(is_first, x, 0.0)
        tbuf[r] = term
        terms[step, r] = term

    for s in others:
        pltpu.make_async_remote_copy(
            tbuf, terms.at[step], t_send, t_recv, device_id={"step": s}, device_id_type=MESH,
        ).start()
    came = terms.at[pl.ds(0, nsteps - 1)]
    pltpu.make_async_copy(came, came, t_recv).wait()
    error = jnp.zeros((LATENT, LANES), F32)
    for r in range(ROWS):
        earlier = jnp.zeros((LATENT, LANES), F32)
        for s in range(nsteps - 1):
            earlier = earlier + jnp.where(s < step, terms[s, r], 0.0)
        adv[0, :, r, :] = earlier + tbuf[r]
        x = traj[0, :, r, :]
        gap = jnp.where(is_first, 0.0, earlier - x)
        error = error + gap * gap
    adv_out = pltpu.make_async_copy(adv, adv_ref, out_sem.at[0])
    adv_out.start()
    send_sums(3, jnp.sum(error, axis=0, keepdims=True))
    whole = jnp.sum(total_sums(3), axis=1, keepdims=True)
    err[...] = whole * (1.0 / (LATENT * height * LANES))
    err_out = pltpu.make_async_copy(err, err_ref, out_sem.at[1])
    err_out.start()

    up.wait_send()
    down.wait_send()
    for c in halo1 + halo2:
        c.wait_send()
    for k in range(4):
        part = others_of(k)
        pltpu.make_async_copy(part, part, ar_send.at[k]).wait()
    pltpu.make_async_copy(came, came, t_send).wait()
    adv_out.wait()
    err_out.wait()


def finish(advanced, error, advanced_out, error_out, adv, err, sem):
    come = [
        pltpu.make_async_copy(advanced, adv, sem.at[0]),
        pltpu.make_async_copy(error, err, sem.at[1]),
    ]
    go = [
        pltpu.make_async_copy(adv, advanced_out, sem.at[2]),
        pltpu.make_async_copy(err, error_out, sem.at[3]),
    ]
    for c in come:
        c.start()
    for c, g in zip(come, go):
        c.wait()
        g.start()
    for g in go:
        g.wait()


def shards(nz, ny, nsteps, trajectory, noise, tsteps, w_in, w_one, w_two, w_out, wt1, wt2, wtp):
    w_in = jnp.transpose(w_in, (0, 1, 3, 2))
    wtp = jnp.transpose(wtp)
    args = (trajectory, noise, tsteps, w_in, w_one, w_two, w_out, wt1, wt2, wtp)
    channels, temb = wt1.shape
    nrow = nz * ny
    height = trajectory.shape[2] * nrow
    vmem = lambda shape, dtype: pltpu.VMEM(shape, dtype)
    scratch = [vmem(a.shape, a.dtype) for a in args] + [
        vmem((LANES, -(-channels // LANES) * LANES), F32),
        vmem((channels, LANES), BF16),
        vmem((3, channels, 3 * channels), BF16),
        vmem((3, channels, 3 * channels), BF16),
        vmem((80, channels), F32),
        vmem((ROWS + 4, LATENT, LANES), F32),
        vmem((48, (ROWS + 2) * LANES), F32),
        vmem((ROWS + 2, channels, LANES), F32),
        vmem((ROWS + 2, channels, LANES), F32),
        vmem((ROWS + 2, channels, LANES), F32),
        vmem((3 * channels, ROWS * LANES), BF16),
        vmem((LANES, LANES), F32),
        vmem((channels, LANES), F32),
        vmem((channels, LANES), F32),
        vmem((channels, LANES), F32),
        vmem((4, 1, LANES), F32),
        vmem((4, nrow, LANES), F32),
        vmem((nsteps, ROWS, LATENT, LANES), F32),
        vmem((ROWS, LATENT, LANES), F32),
        pltpu.SemaphoreType.DMA((len(args),)),
        pltpu.SemaphoreType.DMA((2,)),
        pltpu.SemaphoreType.DMA((2,)),
        pltpu.SemaphoreType.DMA((2, 2)),
        pltpu.SemaphoreType.DMA((2, 2)),
        pltpu.SemaphoreType.DMA((4,)),
        pltpu.SemaphoreType.DMA((4,)),
        pltpu.SemaphoreType.DMA,
        pltpu.SemaphoreType.DMA,
        pltpu.SemaphoreType.REGULAR,
        vmem(trajectory.shape, F32),
        vmem((1, 1), F32),
        pltpu.SemaphoreType.DMA((2,)),
    ]
    advanced, error = pl.pallas_call(
        functools.partial(kernel, nz, ny, nsteps, channels, temb, height),
        out_shape=(
            jax.ShapeDtypeStruct(trajectory.shape, F32),
            jax.ShapeDtypeStruct((1, 1), F32),
        ),
        in_specs=[pl.BlockSpec(memory_space=pltpu.HBM)] * len(args),
        out_specs=(pl.BlockSpec(memory_space=pltpu.HBM),) * 2,
        scratch_shapes=scratch,
        compiler_params=pltpu.CompilerParams(
            collective_id=0, has_side_effects=True, vmem_limit_bytes=56 * 1024 * 1024
        ),
    )(*args)
    advanced, error = pl.pallas_call(
        finish,
        out_shape=(
            jax.ShapeDtypeStruct(trajectory.shape, F32),
            jax.ShapeDtypeStruct((1, 1), F32),
        ),
        in_specs=[pl.BlockSpec(memory_space=pltpu.HBM)] * 2,
        out_specs=(
            pl.BlockSpec(memory_space=pltpu.HBM),
            pl.BlockSpec(memory_space=pltpu.HBM),
        ),
        scratch_shapes=[
            pltpu.VMEM(trajectory.shape, F32),
            pltpu.VMEM((1, 1), F32),
            pltpu.SemaphoreType.DMA((4,)),
        ],
    )(advanced, error)
    return advanced, error.reshape(1)


def solution(mesh):
    nsteps, nrow = mesh.shape["step"], mesh.shape["row"]
    ny = 8 if nrow % 8 == 0 else min(2, nrow)
    place = P("step", None, "row", None)
    return jax.shard_map(
        functools.partial(shards, nrow // ny, ny, nsteps),
        mesh=mesh,
        in_specs=(place, place, P("step", None)) + (P(),) * 7,
        out_specs=(place, P("step")),
        check_vma=False,
    )
```

```python
import functools
import math

import jax
import jax.numpy as jnp
from jax import lax
from jax.experimental import pallas as pl
from jax.experimental.pallas import tpu as pltpu
from jax.sharding import PartitionSpec as P

MESH = pl.DeviceIdType.MESH
F32 = jnp.float32
BF16 = jnp.bfloat16
LATENT = 4
GROUPS = 32
LANES = 128
ROWS = 4
NORM_EPS = 1e-05
NOISE_SHARE = 0.5


def dot(a, b):
    return jnp.dot(a, b, preferred_element_type=F32)


def offsets(nz, ny):
    hops = lambda d, n: min(d, n - d)
    every = [(dz, dy) for dz in range(nz) for dy in range(ny) if (dz, dy) != (0, 0)]
    return sorted(every, key=lambda o: -(hops(o[0], nz) + hops(o[1], ny)))


def silu(x):
    half = 0.5 * x
    return half + half * jnp.tanh(half)


def shifted(x, col):
    if col == 1:
        return x
    lane = lax.broadcasted_iota(jnp.int32, x.shape, x.ndim - 1)
    if col == 0:
        return jnp.where(lane == 0, 0.0, pltpu.roll(x, 1, axis=x.ndim - 1))
    return jnp.where(lane == LANES - 1, 0.0, pltpu.roll(x, LANES - 1, axis=x.ndim - 1))


def kernel(
    nz, ny, nsteps, channels, temb, height,
    traj_h, noise_h, ts_h, w_in_h, w_one_h, w_two_h, w_out_h, wt1_h, wt2_h, wtp_h,
    out_ref,
    traj, noise, ts, w_in, w_one, w_two, w_out, wt1, wt2, wtp,
    win_f, win_m, wone_m, wtwo_m, wout_f,
    xbuf, xcol, h0, h1, rr, acts, vt, mcol, scol, tcol,
    msg, sums, terms, tbuf,
    load_sem, x_send, x_recv, h_send, h_recv, ar_send, ar_recv, t_send, t_recv, line_sem,
):
    nrow = nz * ny
    row = lax.axis_index("row")
    step = lax.axis_index("step")
    mz, my = row // ny, lax.rem(row, ny)
    peers = [
        lax.rem(mz + dz, nz) * ny + lax.rem(my + dy, ny) for dz, dy in offsets(nz, ny)
    ]
    others = [lax.rem(step + d, nsteps) for d in range(1, nsteps)]
    below = lax.rem(row + 1, nrow)
    above = lax.rem(row + nrow - 1, nrow)
    per_group = channels // GROUPS

    terms[...] = jnp.zeros_like(terms)

    column = [lax.rem(mz + d, nz) * ny + my for d in range(1, nz)]
    line = [mz * ny + lax.rem(my + d, ny) for d in range(1, ny)]
    barrier = pltpu.get_barrier_semaphore()
    for p in column + line + [above, below]:
        pl.semaphore_signal(barrier, inc=1, device_id={"row": p}, device_id_type=MESH)
    for s in others:
        pl.semaphore_signal(barrier, inc=1, device_id={"step": s}, device_id_type=MESH)

    loads = [
        (traj_h, traj), (noise_h, noise), (ts_h, ts), (w_in_h, w_in), (w_one_h, w_one),
        (wt1_h, wt1), (wt2_h, wt2), (wtp_h, wtp), (w_two_h, w_two), (w_out_h, w_out),
    ]
    copies = [
        pltpu.make_async_copy(src, dst, load_sem.at[i]) for i, (src, dst) in enumerate(loads)
    ]
    for c in copies:
        c.start()
    (c_traj, c_noise, c_ts, c_win, c_wone, c_wt1, c_wt2, c_wtp, c_wtwo, c_wout) = copies

    c_traj.wait()
    for r in range(ROWS):
        xbuf[2 + r] = traj[0, :, r, :]

    xcol[...] = jnp.zeros_like(xcol)
    win_f[...] = jnp.zeros_like(win_f)
    c_win.wait()
    for p in range(3):
        for q in range(3):
            tap = 4 * (3 * p + q)
            win_f[tap : tap + 4, :channels] = w_in[p, q].astype(F32)
    win_m[...] = jnp.transpose(win_f[...])[:channels].astype(BF16)

    pl.semaphore_wait(barrier, nz - 1 + ny - 1 + 2 + nsteps - 1)

    up = pltpu.make_async_remote_copy(
        xbuf.at[pl.ds(2, 2)], xbuf.at[pl.ds(6, 2)], x_send.at[0], x_recv.at[0],
        device_id={"row": above}, device_id_type=MESH,
    )
    down = pltpu.make_async_remote_copy(
        xbuf.at[pl.ds(4, 2)], xbuf.at[pl.ds(0, 2)], x_send.at[1], x_recv.at[1],
        device_id={"row": below}, device_id_type=MESH,
    )
    up.start()
    down.start()
    for p in column:
        pl.semaphore_signal(line_sem, inc=1, device_id={"row": p}, device_id_type=MESH)

    def merge(weights, merged):
        for q in range(3):
            merged[q] = jnp.concatenate([weights[p, q] for p in range(3)], axis=1)

    c_wone.wait()
    merge(w_one, wone_m)

    is_top = row == 0
    is_bottom = row == nrow - 1

    def send_sums(k, line):
        msg[k] = line
        sums[k, pl.ds(row, 1), :] = line
        for p in peers:
            pltpu.make_async_remote_copy(
                msg.at[k], sums.at[k, pl.ds(row, 1), :], ar_send.at[k], ar_recv.at[k],
                device_id={"row": p}, device_id_type=MESH,
            ).start()

    def others_of(k):
        return sums.at[k, pl.ds(0, nrow - 1), :]

    def total_sums(k):
        part = others_of(k)
        pltpu.make_async_copy(part, part, ar_recv.at[k]).wait()
        return jnp.sum(sums[k], axis=0, keepdims=True)

    group_of = lax.broadcasted_iota(jnp.int32, (GROUPS, channels), 0) * per_group
    channel = lax.broadcasted_iota(jnp.int32, (GROUPS, channels), 1)
    members = jnp.where(
        (channel >= group_of) & (channel < group_of + per_group), 1.0, 0.0
    ).astype(BF16)

    def group_line(rows):
        total = functools.reduce(lambda a, b: a + b, rows)
        square = functools.reduce(lambda a, b: a + b, [v * v for v in rows])
        lane = lax.broadcasted_iota(jnp.int32, total.shape, 1)
        both = jnp.where(
            lane < LANES // 2,
            total + pltpu.roll(total, LANES // 2, axis=1),
            square + pltpu.roll(square, LANES // 2, axis=1),
        )
        high = both.astype(BF16)
        rest = both - high.astype(F32)
        mid = rest.astype(BF16)
        low = (rest - mid.astype(F32)).astype(BF16)
        grouped = dot(members, jnp.concatenate([high, mid, low], axis=1))
        grouped = grouped[:, :LANES] + grouped[:, LANES : 2 * LANES] + grouped[:, 2 * LANES :]
        stacked = jnp.concatenate(
            [grouped, pltpu.roll(grouped, LANES // 2, axis=1), jnp.zeros((64, LANES), F32)], axis=0
        )
        return jnp.sum(jnp.transpose(stacked)[: LANES // 2], axis=0, keepdims=True)

    count = per_group * height * LANES

    def norm_columns(k):
        total = total_sums(k) * (1.0 / count)
        columns = jnp.transpose(jnp.broadcast_to(total, (LANES, LANES)))
        mean, square = columns[:GROUPS], columns[GROUPS : 2 * GROUPS]
        vt[:GROUPS, :] = mean
        vt[GROUPS:, :] = 0.5 * lax.rsqrt(square - mean * mean + NORM_EPS)
        sub = lax.broadcasted_iota(jnp.int32, (8, LANES), 0)
        for first, target in ((0, mcol), (GROUPS, scol)):
            for j in range(channels // 8):
                low, high = 8 * j // per_group, (8 * j + 7) // per_group
                value = jnp.broadcast_to(vt[first + low : first + low + 1, :], (8, LANES))
                if high != low:
                    other = jnp.broadcast_to(vt[first + high : first + high + 1, :], (8, LANES))
                    value = jnp.where(sub < high * per_group - 8 * j, value, other)
                target[8 * j : 8 * j + 8, :] = value

    def activate(source, r):
        half = (source[r] - mcol[...]) * scol[...]
        act = half + half * jnp.tanh(half)
        if r == 0:
            act = jnp.where(is_top, 0.0, act)
        if r == ROWS + 1:
            act = jnp.where(is_bottom, 0.0, act)
        return act.astype(BF16)

    def place(r, act):
        for p in range(3):
            if 0 <= r - p < ROWS:
                acts[p * channels : (p + 1) * channels, (r - p) * LANES : (r - p + 1) * LANES] = act

    def conv(merged, source, finish):
        for half in range(ROWS // 2):
            for r in range(ROWS) if half == 0 else (ROWS, ROWS + 1):
                place(r, activate(source, r))
            x = acts[:, half * 2 * LANES : (half + 1) * 2 * LANES]
            y = [dot(merged[q], x) for q in range(3)]
            for i in range(2):
                cut = slice(i * LANES, (i + 1) * LANES)
                finish(2 * half + i, sum(shifted(y[q][:, cut], q) for q in range(3)))

    def halo_copies(buf, k):
        return [
            pltpu.make_async_remote_copy(
                buf.at[1], buf.at[ROWS + 1], h_send.at[k, 0], h_recv.at[k, 0],
                device_id={"row": above}, device_id_type=MESH,
            ),
            pltpu.make_async_remote_copy(
                buf.at[ROWS], buf.at[0], h_send.at[k, 1], h_recv.at[k, 1],
                device_id={"row": below}, device_id_type=MESH,
            ),
        ]

    up.wait_recv()
    down.wait_recv()
    for r in range(ROWS + 4):
        x = xbuf[r]
        if r < 2:
            x = jnp.where(is_top, 0.0, x)
        if r >= ROWS + 2:
            x = jnp.where(is_bottom, 0.0, x)
        for q in range(3):
            moved = shifted(x, q)
            for p in range(3):
                if 0 <= r - p < ROWS + 2:
                    tap = 4 * (3 * p + q)
                    xcol[tap : tap + 4, (r - p) * LANES : (r - p + 1) * LANES] = moved
    first = dot(win_m[:, :48], xcol[...].astype(BF16))
    for r in range(ROWS + 2):
        h0[r] = first[:, r * LANES : (r + 1) * LANES]
    pl.semaphore_wait(line_sem, nz - 1)
    send_sums(0, group_line([h0[r] for r in range(1, ROWS + 1)]))

    c_ts.wait()
    times = ts[...].astype(F32)
    level = jnp.broadcast_to(times[:, 0:1], (1, LANES))
    level_next = jnp.broadcast_to(times[:, 1:2], (1, LANES))
    c_wt1.wait()
    half = channels // 2
    lane = lax.broadcasted_iota(jnp.int32, (LANES, channels), 1)
    place_of = jnp.where(lane < half, lane, lane - half).astype(F32)
    freq = jnp.exp(-math.log(10000.0) * place_of / half)
    angle = jnp.broadcast_to(times[:, 0:1], (LANES, channels)) * freq
    embed = jnp.where(lane < half, jnp.cos(angle), jnp.sin(angle)).astype(BF16)
    hidden = silu(dot(embed, wt1[...])).astype(BF16)
    c_wt2.wait()
    second = silu(dot(hidden, wt2[...])).astype(BF16)
    c_wtp.wait()
    tcol[...] = lax.dot_general(
        wtp[...], second, (((1,), (1,)), ((), ())), preferred_element_type=F32
    )

    c_wtwo.wait()
    merge(w_two, wtwo_m)
    c_wout.wait()
    wout_f[...] = jnp.zeros_like(wout_f)
    for p in range(3):
        for q in range(3):
            tap = 8 * (3 * p + q)
            wout_f[tap : tap + 4, :] = w_out[p, q].astype(F32)

    def alpha_bar(t):
        return jnp.cos((t / 1000.0 + 0.008) / 1.008 * (math.pi / 2)) ** 2

    now, after = alpha_bar(level), alpha_bar(level_next)
    sigma = NOISE_SHARE * jnp.sqrt((1.0 - after) / (1.0 - now) * (1.0 - now / after))
    keep_x = jnp.sqrt(after / now)
    keep_e = jnp.sqrt(1.0 - after - sigma * sigma) - jnp.sqrt(after) * jnp.sqrt(
        1.0 - now
    ) / jnp.sqrt(now)

    norm_columns(0)

    def finish_one(r, value):
        h1[1 + r] = value + tcol[...]

    conv(wone_m, h0, finish_one)
    halo1 = halo_copies(h1, 0)
    send_sums(1, group_line([h1[r] for r in range(1, ROWS + 1)]))
    for c in halo1:
        c.start()

    norm_columns(1)
    for c in halo1:
        c.wait_recv()

    def finish_two(r, value):
        rr[1 + r] = value + h0[1 + r]

    conv(wtwo_m, h1, finish_two)
    halo2 = halo_copies(rr, 1)
    send_sums(2, group_line([rr[r] for r in range(1, ROWS + 1)]))
    for c in halo2:
        c.start()

    c_noise.wait()
    norm_columns(2)
    for c in halo2:
        c.wait_recv()
    a3 = jnp.concatenate([activate(rr, r) for r in range(ROWS + 2)], axis=1)
    y = dot(wout_f[...].astype(BF16), a3)
    is_first = step == 0
    for r in range(ROWS):
        eps = jnp.zeros((8, LANES), F32)
        for q in range(3):
            column = jnp.zeros((8, LANES), F32)
            for p in range(3):
                tap = 8 * (3 * p + q)
                column += y[tap : tap + 8, (r + p) * LANES : (r + p + 1) * LANES]
            eps += shifted(column, q)
        x = traj[0, :, r, :]
        term = keep_x * x + keep_e * eps[:LATENT] + sigma * noise[0, :, r, :] - x
        term = term + jnp.where(is_first, x, 0.0)
        tbuf[r] = term

    def to_later(d):
        return pltpu.make_async_remote_copy(
            tbuf, terms.at[step], t_send.at[d - 1], t_recv.at[step],
            device_id={"step": lax.rem(step + d, nsteps)}, device_id_type=MESH,
        )

    for d in range(1, nsteps):
        @pl.when(step + d < nsteps)
        def _():
            to_later(d).start()
    for s in range(nsteps - 1):
        @pl.when(s < step)
        def _():
            pltpu.make_async_copy(tbuf, tbuf, t_recv.at[s]).wait()
    error = jnp.zeros((LATENT, LANES), F32)
    for r in range(ROWS):
        earlier = jnp.zeros((LATENT, LANES), F32)
        for s in range(nsteps - 1):
            earlier = earlier + terms[s, r]
        out_ref[0, :LATENT, r, :] = earlier + tbuf[r]
        x = traj[0, :, r, :]
        gap = jnp.where(is_first, 0.0, earlier - x)
        error = error + gap * gap
    send_sums(3, jnp.sum(error, axis=0, keepdims=True))
    whole = jnp.sum(total_sums(3), axis=1, keepdims=True)
    out_ref[0, LATENT] = jnp.broadcast_to(
        whole * (1.0 / (LATENT * height * LANES)), (ROWS, LANES)
    )

    up.wait_send()
    down.wait_send()
    for c in halo1 + halo2:
        c.wait_send()
    for k in range(4):
        part = others_of(k)
        pltpu.make_async_copy(part, part, ar_send.at[k]).wait()
    for d in range(1, nsteps):
        @pl.when(step + d < nsteps)
        def _():
            to_later(d).wait_send()


def finish(both, advanced_out, error_out, error, sem):
    copies = [
        pltpu.make_async_copy(both.at[:, pl.ds(0, LATENT)], advanced_out, sem.at[0]),
        pltpu.make_async_copy(error, error_out, sem.at[1]),
    ]
    copies[0].start()
    error[...] = both[0, LATENT, 0:1, 0:1]
    copies[1].start()
    for c in copies:
        c.wait()


def shards(nz, ny, nsteps, trajectory, noise, tsteps, w_in, w_one, w_two, w_out, wt1, wt2, wtp):
    w_in = jnp.transpose(w_in, (0, 1, 3, 2))
    wtp = jnp.transpose(wtp)
    args = (trajectory, noise, tsteps, w_in, w_one, w_two, w_out, wt1, wt2, wtp)
    channels, temb = wt1.shape
    nrow = nz * ny
    height = trajectory.shape[2] * nrow
    vmem = lambda shape, dtype: pltpu.VMEM(shape, dtype)
    scratch = [vmem(a.shape, a.dtype) for a in args] + [
        vmem((LANES, -(-channels // LANES) * LANES), F32),
        vmem((channels, LANES), BF16),
        vmem((3, channels, 3 * channels), BF16),
        vmem((3, channels, 3 * channels), BF16),
        vmem((80, channels), F32),
        vmem((ROWS + 4, LATENT, LANES), F32),
        vmem((48, (ROWS + 2) * LANES), F32),
        vmem((ROWS + 2, channels, LANES), F32),
        vmem((ROWS + 2, channels, LANES), F32),
        vmem((ROWS + 2, channels, LANES), F32),
        vmem((3 * channels, ROWS * LANES), BF16),
        vmem((2 * GROUPS, LANES), F32),
        vmem((channels, LANES), F32),
        vmem((channels, LANES), F32),
        vmem((channels, LANES), F32),
        vmem((4, 1, LANES), F32),
        vmem((4, nrow, LANES), F32),
        vmem((nsteps - 1, ROWS, LATENT, LANES), F32),
        vmem((ROWS, LATENT, LANES), F32),
        pltpu.SemaphoreType.DMA((len(args),)),
        pltpu.SemaphoreType.DMA((2,)),
        pltpu.SemaphoreType.DMA((2,)),
        pltpu.SemaphoreType.DMA((2, 2)),
        pltpu.SemaphoreType.DMA((2, 2)),
        pltpu.SemaphoreType.DMA((4,)),
        pltpu.SemaphoreType.DMA((4,)),
        pltpu.SemaphoreType.DMA((nsteps - 1,)),
        pltpu.SemaphoreType.DMA((nsteps - 1,)),
        pltpu.SemaphoreType.REGULAR,
    ]
    both = pl.pallas_call(
        functools.partial(kernel, nz, ny, nsteps, channels, temb, height),
        out_shape=pltpu.VMEM((1, LATENT + 1, ROWS, LANES), F32),
        in_specs=[pl.BlockSpec(memory_space=pltpu.HBM)] * len(args),
        out_specs=pl.BlockSpec(memory_space=pltpu.VMEM),
        scratch_shapes=scratch,
        compiler_params=pltpu.CompilerParams(
            collective_id=0, has_side_effects=True, vmem_limit_bytes=56 * 1024 * 1024
        ),
    )(*args)
    advanced, error = pl.pallas_call(
        finish,
        out_shape=(
            jax.ShapeDtypeStruct(trajectory.shape, F32),
            jax.ShapeDtypeStruct((1, 1), F32),
        ),
        in_specs=[pl.BlockSpec(memory_space=pltpu.VMEM)],
        out_specs=(pl.BlockSpec(memory_space=pltpu.HBM),) * 2,
        scratch_shapes=[pltpu.VMEM((1, 1), F32), pltpu.SemaphoreType.DMA((2,))],
    )(pltpu.with_memory_space_constraint(both, pltpu.VMEM))
    return advanced, error.reshape(1)


def solution(mesh):
    nsteps, nrow = mesh.shape["step"], mesh.shape["row"]
    ny = 8 if nrow % 8 == 0 else min(2, nrow)
    place = P("step", None, "row", None)
    return jax.shard_map(
        functools.partial(shards, nrow // ny, ny, nsteps),
        mesh=mesh,
        in_specs=(place, place, P("step", None)) + (P(),) * 7,
        out_specs=(place, P("step")),
        check_vma=False,
    )
```

```python
import functools
import math

import jax
import jax.numpy as jnp
from jax import lax
from jax.experimental import pallas as pl
from jax.experimental.pallas import tpu as pltpu
from jax.sharding import PartitionSpec as P

MESH = pl.DeviceIdType.MESH
F32 = jnp.float32
BF16 = jnp.bfloat16
LATENT = 4
GROUPS = 32
LANES = 128
ROWS = 4
NORM_EPS = 1e-05
NOISE_SHARE = 0.5


def dot(a, b):
    return jnp.dot(a, b, preferred_element_type=F32)


def offsets(nz, ny):
    hops = lambda d, n: min(d, n - d)
    every = [(dz, dy) for dz in range(nz) for dy in range(ny) if (dz, dy) != (0, 0)]
    return sorted(every, key=lambda o: -(hops(o[0], nz) + hops(o[1], ny)))


def silu(x):
    half = 0.5 * x
    return half + half * jnp.tanh(half)


def shifted(x, col):
    if col == 1:
        return x
    lane = lax.broadcasted_iota(jnp.int32, x.shape, x.ndim - 1)
    if col == 0:
        return jnp.where(lane == 0, 0.0, pltpu.roll(x, 1, axis=x.ndim - 1))
    return jnp.where(lane == LANES - 1, 0.0, pltpu.roll(x, LANES - 1, axis=x.ndim - 1))


def kernel(
    nz, ny, nsteps, channels, temb, height,
    traj_h, noise_h, ts_h, w_in_h, w_one_h, w_two_h, w_out_h, wt1_h, wt2_h, wtp_h,
    out_ref,
    traj, noise, ts, w_in, w_one, w_two, w_out, wt1, wt2, wtp,
    win_f, win_m, wone_m, wtwo_m, wout_f,
    xbuf, xcol, h0, h1, rr, acts, vt, mcol, scol, tcol,
    msg, sums, terms, tbuf,
    load_sem, x_send, x_recv, h_send, h_recv, ar_send, ar_recv, t_send, t_recv, line_sem, end_sem,
):
    nrow = nz * ny
    row = lax.axis_index("row")
    step = lax.axis_index("step")
    mz, my = row // ny, lax.rem(row, ny)
    peers = [
        lax.rem(mz + dz, nz) * ny + lax.rem(my + dy, ny) for dz, dy in offsets(nz, ny)
    ]
    others = [lax.rem(step + d, nsteps) for d in range(1, nsteps)]
    below = lax.rem(row + 1, nrow)
    above = lax.rem(row + nrow - 1, nrow)
    per_group = channels // GROUPS

    terms[...] = jnp.zeros_like(terms)

    def at_end(y):
        return (y == 0) | (y == ny - 1) if ny >= 4 else y < 0

    column = [lax.rem(mz + d, nz) * ny + my for d in range(1, nz)]
    line = [mz * ny + lax.rem(my + d, ny) for d in range(1, ny)]
    barrier = pltpu.get_barrier_semaphore()
    for p in column + [above, below]:
        pl.semaphore_signal(barrier, inc=1, device_id={"row": p}, device_id_type=MESH)
    for d, p in enumerate(line, 1):
        @pl.when(jnp.logical_not(at_end(lax.rem(my + d, ny))))
        def _():
            pl.semaphore_signal(barrier, inc=1, device_id={"row": p}, device_id_type=MESH)
    for s in others:
        pl.semaphore_signal(barrier, inc=1, device_id={"step": s}, device_id_type=MESH)

    loads = [
        (traj_h, traj), (noise_h, noise), (ts_h, ts), (w_in_h, w_in), (w_one_h, w_one),
        (wt1_h, wt1), (wt2_h, wt2), (wtp_h, wtp), (w_two_h, w_two), (w_out_h, w_out),
    ]
    copies = [
        pltpu.make_async_copy(src, dst, load_sem.at[i]) for i, (src, dst) in enumerate(loads)
    ]
    for c in copies:
        c.start()
    (c_traj, c_noise, c_ts, c_win, c_wone, c_wt1, c_wt2, c_wtp, c_wtwo, c_wout) = copies

    c_traj.wait()
    for r in range(ROWS):
        xbuf[2 + r] = traj[0, :, r, :]

    xcol[...] = jnp.zeros_like(xcol)
    win_f[...] = jnp.zeros_like(win_f)
    c_win.wait()
    for p in range(3):
        for q in range(3):
            tap = 4 * (3 * p + q)
            win_f[tap : tap + 4, :channels] = w_in[p, q].astype(F32)
    win_m[...] = jnp.transpose(win_f[...])[:channels].astype(BF16)

    here = at_end(my)
    pl.semaphore_wait(barrier, nz - 1 + 2 + nsteps - 1 + jnp.where(here, 0, ny - 1))

    up = pltpu.make_async_remote_copy(
        xbuf.at[pl.ds(2, 2)], xbuf.at[pl.ds(6, 2)], x_send.at[0], x_recv.at[0],
        device_id={"row": above}, device_id_type=MESH,
    )
    down = pltpu.make_async_remote_copy(
        xbuf.at[pl.ds(4, 2)], xbuf.at[pl.ds(0, 2)], x_send.at[1], x_recv.at[1],
        device_id={"row": below}, device_id_type=MESH,
    )
    up.start()
    down.start()
    if ny >= 4:
        @pl.when((my == 1) | (my == ny - 2))
        def _():
            pl.semaphore_signal(
                end_sem, inc=1, device_id={"row": jnp.where(my == 1, above, below)},
                device_id_type=MESH,
            )

        @pl.when(here)
        def _():
            pl.semaphore_wait(end_sem, 1)

    for p in column:
        pl.semaphore_signal(line_sem, inc=1, device_id={"row": p}, device_id_type=MESH)

    def merge(weights, merged):
        for q in range(3):
            merged[q] = jnp.concatenate([weights[p, q] for p in range(3)], axis=1)

    c_wone.wait()
    merge(w_one, wone_m)

    is_top = row == 0
    is_bottom = row == nrow - 1

    def send_sums(k, line):
        msg[k] = line
        sums[k, pl.ds(row, 1), :] = line
        for p in peers:
            pltpu.make_async_remote_copy(
                msg.at[k], sums.at[k, pl.ds(row, 1), :], ar_send.at[k], ar_recv.at[k],
                device_id={"row": p}, device_id_type=MESH,
            ).start()

    def others_of(k):
        return sums.at[k, pl.ds(0, nrow - 1), :]

    def total_sums(k):
        part = others_of(k)
        pltpu.make_async_copy(part, part, ar_recv.at[k]).wait()
        return jnp.sum(sums[k], axis=0, keepdims=True)

    group_of = lax.broadcasted_iota(jnp.int32, (GROUPS, channels), 0) * per_group
    channel = lax.broadcasted_iota(jnp.int32, (GROUPS, channels), 1)
    members = jnp.where(
        (channel >= group_of) & (channel < group_of + per_group), 1.0, 0.0
    ).astype(BF16)

    def group_line(rows):
        total = functools.reduce(lambda a, b: a + b, rows)
        square = functools.reduce(lambda a, b: a + b, [v * v for v in rows])
        lane = lax.broadcasted_iota(jnp.int32, total.shape, 1)
        both = jnp.where(
            lane < LANES // 2,
            total + pltpu.roll(total, LANES // 2, axis=1),
            square + pltpu.roll(square, LANES // 2, axis=1),
        )
        high = both.astype(BF16)
        rest = both - high.astype(F32)
        mid = rest.astype(BF16)
        low = (rest - mid.astype(F32)).astype(BF16)
        grouped = dot(members, jnp.concatenate([high, mid, low], axis=1))
        grouped = grouped[:, :LANES] + grouped[:, LANES : 2 * LANES] + grouped[:, 2 * LANES :]
        stacked = jnp.concatenate(
            [grouped, pltpu.roll(grouped, LANES // 2, axis=1), jnp.zeros((64, LANES), F32)], axis=0
        )
        return jnp.sum(jnp.transpose(stacked)[: LANES // 2], axis=0, keepdims=True)

    count = per_group * height * LANES

    def norm_columns(k):
        total = total_sums(k) * (1.0 / count)
        columns = jnp.transpose(jnp.broadcast_to(total, (LANES, LANES)))
        mean, square = columns[:GROUPS], columns[GROUPS : 2 * GROUPS]
        vt[:GROUPS, :] = mean
        vt[GROUPS:, :] = 0.5 * lax.rsqrt(square - mean * mean + NORM_EPS)
        sub = lax.broadcasted_iota(jnp.int32, (8, LANES), 0)
        for first, target in ((0, mcol), (GROUPS, scol)):
            for j in range(channels // 8):
                low, high = 8 * j // per_group, (8 * j + 7) // per_group
                value = jnp.broadcast_to(vt[first + low : first + low + 1, :], (8, LANES))
                if high != low:
                    other = jnp.broadcast_to(vt[first + high : first + high + 1, :], (8, LANES))
                    value = jnp.where(sub < high * per_group - 8 * j, value, other)
                target[8 * j : 8 * j + 8, :] = value

    def activate(source, r):
        half = (source[r] - mcol[...]) * scol[...]
        act = half + half * jnp.tanh(half)
        if r == 0:
            act = jnp.where(is_top, 0.0, act)
        if r == ROWS + 1:
            act = jnp.where(is_bottom, 0.0, act)
        return act.astype(BF16)

    def place(r, act):
        for p in range(3):
            if 0 <= r - p < ROWS:
                acts[p * channels : (p + 1) * channels, (r - p) * LANES : (r - p + 1) * LANES] = act

    def conv(merged, source, finish):
        for half in range(ROWS // 2):
            for r in range(ROWS) if half == 0 else (ROWS, ROWS + 1):
                place(r, activate(source, r))
            x = acts[:, half * 2 * LANES : (half + 1) * 2 * LANES]
            y = [dot(merged[q], x) for q in range(3)]
            for i in range(2):
                cut = slice(i * LANES, (i + 1) * LANES)
                finish(2 * half + i, sum(shifted(y[q][:, cut], q) for q in range(3)))

    def halo_copies(buf, k):
        return [
            pltpu.make_async_remote_copy(
                buf.at[1], buf.at[ROWS + 1], h_send.at[k, 0], h_recv.at[k, 0],
                device_id={"row": above}, device_id_type=MESH,
            ),
            pltpu.make_async_remote_copy(
                buf.at[ROWS], buf.at[0], h_send.at[k, 1], h_recv.at[k, 1],
                device_id={"row": below}, device_id_type=MESH,
            ),
        ]

    up.wait_recv()
    down.wait_recv()
    for r in range(ROWS + 4):
        x = xbuf[r]
        if r < 2:
            x = jnp.where(is_top, 0.0, x)
        if r >= ROWS + 2:
            x = jnp.where(is_bottom, 0.0, x)
        for q in range(3):
            moved = shifted(x, q)
            for p in range(3):
                if 0 <= r - p < ROWS + 2:
                    tap = 4 * (3 * p + q)
                    xcol[tap : tap + 4, (r - p) * LANES : (r - p + 1) * LANES] = moved
    first = dot(win_m[:, :48], xcol[...].astype(BF16))
    for r in range(ROWS + 2):
        h0[r] = first[:, r * LANES : (r + 1) * LANES]
    pl.semaphore_wait(line_sem, nz - 1)
    send_sums(0, group_line([h0[r] for r in range(1, ROWS + 1)]))

    c_ts.wait()
    times = ts[...].astype(F32)
    level = jnp.broadcast_to(times[:, 0:1], (1, LANES))
    level_next = jnp.broadcast_to(times[:, 1:2], (1, LANES))
    c_wt1.wait()
    half = channels // 2
    lane = lax.broadcasted_iota(jnp.int32, (LANES, channels), 1)
    place_of = jnp.where(lane < half, lane, lane - half).astype(F32)
    freq = jnp.exp(-math.log(10000.0) * place_of / half)
    angle = jnp.broadcast_to(times[:, 0:1], (LANES, channels)) * freq
    embed = jnp.where(lane < half, jnp.cos(angle), jnp.sin(angle)).astype(BF16)
    hidden = silu(dot(embed, wt1[...])).astype(BF16)
    c_wt2.wait()
    second = silu(dot(hidden, wt2[...])).astype(BF16)
    c_wtp.wait()
    tcol[...] = lax.dot_general(
        wtp[...], second, (((1,), (1,)), ((), ())), preferred_element_type=F32
    )

    c_wtwo.wait()
    merge(w_two, wtwo_m)
    c_wout.wait()
    wout_f[...] = jnp.zeros_like(wout_f)
    for p in range(3):
        for q in range(3):
            tap = 8 * (3 * p + q)
            wout_f[tap : tap + 4, :] = w_out[p, q].astype(F32)

    def alpha_bar(t):
        return jnp.cos((t / 1000.0 + 0.008) / 1.008 * (math.pi / 2)) ** 2

    now, after = alpha_bar(level), alpha_bar(level_next)
    sigma = NOISE_SHARE * jnp.sqrt((1.0 - after) / (1.0 - now) * (1.0 - now / after))
    keep_x = jnp.sqrt(after / now)
    keep_e = jnp.sqrt(1.0 - after - sigma * sigma) - jnp.sqrt(after) * jnp.sqrt(
        1.0 - now
    ) / jnp.sqrt(now)

    norm_columns(0)

    def finish_one(r, value):
        h1[1 + r] = value + tcol[...]

    conv(wone_m, h0, finish_one)
    halo1 = halo_copies(h1, 0)
    send_sums(1, group_line([h1[r] for r in range(1, ROWS + 1)]))
    for c in halo1:
        c.start()

    norm_columns(1)
    for c in halo1:
        c.wait_recv()

    def finish_two(r, value):
        rr[1 + r] = value + h0[1 + r]

    conv(wtwo_m, h1, finish_two)
    halo2 = halo_copies(rr, 1)
    send_sums(2, group_line([rr[r] for r in range(1, ROWS + 1)]))
    for c in halo2:
        c.start()

    c_noise.wait()
    norm_columns(2)
    for c in halo2:
        c.wait_recv()
    a3 = jnp.concatenate([activate(rr, r) for r in range(ROWS + 2)], axis=1)
    y = dot(wout_f[...].astype(BF16), a3)
    is_first = step == 0
    for r in range(ROWS):
        eps = jnp.zeros((8, LANES), F32)
        for q in range(3):
            column = jnp.zeros((8, LANES), F32)
            for p in range(3):
                tap = 8 * (3 * p + q)
                column += y[tap : tap + 8, (r + p) * LANES : (r + p + 1) * LANES]
            eps += shifted(column, q)
        x = traj[0, :, r, :]
        term = keep_x * x + keep_e * eps[:LATENT] + sigma * noise[0, :, r, :] - x
        term = term + jnp.where(is_first, x, 0.0)
        tbuf[r] = term

    def to_later(d):
        return pltpu.make_async_remote_copy(
            tbuf, terms.at[step], t_send.at[d - 1], t_recv.at[step],
            device_id={"step": lax.rem(step + d, nsteps)}, device_id_type=MESH,
        )

    for d in range(nsteps - 1, 0, -1):
        @pl.when(step + d < nsteps)
        def _():
            to_later(d).start()
    for s in range(nsteps - 1):
        @pl.when(s < step)
        def _():
            pltpu.make_async_copy(tbuf, tbuf, t_recv.at[s]).wait()
    error = jnp.zeros((LATENT, LANES), F32)
    for r in range(ROWS):
        earlier = jnp.zeros((LATENT, LANES), F32)
        for s in range(nsteps - 1):
            earlier = earlier + terms[s, r]
        out_ref[0, :LATENT, r, :] = earlier + tbuf[r]
        x = traj[0, :, r, :]
        gap = jnp.where(is_first, 0.0, earlier - x)
        error = error + gap * gap
    send_sums(3, jnp.sum(error, axis=0, keepdims=True))
    whole = jnp.sum(total_sums(3), axis=1, keepdims=True)
    out_ref[0, LATENT] = jnp.broadcast_to(
        whole * (1.0 / (LATENT * height * LANES)), (ROWS, LANES)
    )

    up.wait_send()
    down.wait_send()
    for c in halo1 + halo2:
        c.wait_send()
    for k in range(4):
        part = others_of(k)
        pltpu.make_async_copy(part, part, ar_send.at[k]).wait()
    for d in range(1, nsteps):
        @pl.when(step + d < nsteps)
        def _():
            to_later(d).wait_send()


def finish(both, advanced_out, error_out, error, sem):
    copies = [
        pltpu.make_async_copy(both.at[:, pl.ds(0, LATENT)], advanced_out, sem.at[0]),
        pltpu.make_async_copy(error, error_out, sem.at[1]),
    ]
    copies[0].start()
    error[...] = both[0, LATENT, 0:1, 0:1]
    copies[1].start()
    for c in copies:
        c.wait()


def shards(nz, ny, nsteps, trajectory, noise, tsteps, w_in, w_one, w_two, w_out, wt1, wt2, wtp):
    w_in = jnp.transpose(w_in, (0, 1, 3, 2))
    wtp = jnp.transpose(wtp)
    args = (trajectory, noise, tsteps, w_in, w_one, w_two, w_out, wt1, wt2, wtp)
    channels, temb = wt1.shape
    nrow = nz * ny
    height = trajectory.shape[2] * nrow
    vmem = lambda shape, dtype: pltpu.VMEM(shape, dtype)
    scratch = [vmem(a.shape, a.dtype) for a in args] + [
        vmem((LANES, -(-channels // LANES) * LANES), F32),
        vmem((channels, LANES), BF16),
        vmem((3, channels, 3 * channels), BF16),
        vmem((3, channels, 3 * channels), BF16),
        vmem((80, channels), F32),
        vmem((ROWS + 4, LATENT, LANES), F32),
        vmem((48, (ROWS + 2) * LANES), F32),
        vmem((ROWS + 2, channels, LANES), F32),
        vmem((ROWS + 2, channels, LANES), F32),
        vmem((ROWS + 2, channels, LANES), F32),
        vmem((3 * channels, ROWS * LANES), BF16),
        vmem((2 * GROUPS, LANES), F32),
        vmem((channels, LANES), F32),
        vmem((channels, LANES), F32),
        vmem((channels, LANES), F32),
        vmem((4, 1, LANES), F32),
        vmem((4, nrow, LANES), F32),
        vmem((nsteps - 1, ROWS, LATENT, LANES), F32),
        vmem((ROWS, LATENT, LANES), F32),
        pltpu.SemaphoreType.DMA((len(args),)),
        pltpu.SemaphoreType.DMA((2,)),
        pltpu.SemaphoreType.DMA((2,)),
        pltpu.SemaphoreType.DMA((2, 2)),
        pltpu.SemaphoreType.DMA((2, 2)),
        pltpu.SemaphoreType.DMA((4,)),
        pltpu.SemaphoreType.DMA((4,)),
        pltpu.SemaphoreType.DMA((nsteps - 1,)),
        pltpu.SemaphoreType.DMA((nsteps - 1,)),
        pltpu.SemaphoreType.REGULAR,
        pltpu.SemaphoreType.REGULAR,
    ]
    both = pl.pallas_call(
        functools.partial(kernel, nz, ny, nsteps, channels, temb, height),
        out_shape=pltpu.VMEM((1, LATENT + 1, ROWS, LANES), F32),
        in_specs=[pl.BlockSpec(memory_space=pltpu.HBM)] * len(args),
        out_specs=pl.BlockSpec(memory_space=pltpu.VMEM),
        scratch_shapes=scratch,
        compiler_params=pltpu.CompilerParams(
            collective_id=0, has_side_effects=True, vmem_limit_bytes=56 * 1024 * 1024
        ),
    )(*args)
    advanced, error = pl.pallas_call(
        finish,
        out_shape=(
            jax.ShapeDtypeStruct(trajectory.shape, F32),
            jax.ShapeDtypeStruct((1, 1), F32),
        ),
        in_specs=[pl.BlockSpec(memory_space=pltpu.VMEM)],
        out_specs=(pl.BlockSpec(memory_space=pltpu.HBM),) * 2,
        scratch_shapes=[pltpu.VMEM((1, 1), F32), pltpu.SemaphoreType.DMA((2,))],
    )(pltpu.with_memory_space_constraint(both, pltpu.VMEM))
    return advanced, error.reshape(1)


def solution(mesh):
    nsteps, nrow = mesh.shape["step"], mesh.shape["row"]
    ny = 8 if nrow % 64 == 0 else max(1, nrow // 2)
    place = P("step", None, "row", None)
    return jax.shard_map(
        functools.partial(shards, nrow // ny, ny, nsteps),
        mesh=mesh,
        in_specs=(place, place, P("step", None)) + (P(),) * 7,
        out_specs=(place, P("step")),
        check_vma=False,
    )
```

```python
import functools
import math

import jax
import jax.numpy as jnp
from jax import lax
from jax.experimental import pallas as pl
from jax.experimental.pallas import tpu as pltpu
from jax.sharding import PartitionSpec as P

MESH = pl.DeviceIdType.MESH
F32 = jnp.float32
BF16 = jnp.bfloat16
LATENT = 4
GROUPS = 32
LANES = 128
ROWS = 4
NORM_EPS = 1e-05
NOISE_SHARE = 0.5


def dot(a, b):
    return jnp.dot(a, b, preferred_element_type=F32)


def offsets(nz, ny):
    hops = lambda d, n: min(d, n - d)
    every = [(dz, dy) for dz in range(nz) for dy in range(ny) if (dz, dy) != (0, 0)]
    return sorted(every, key=lambda o: -(hops(o[0], nz) + hops(o[1], ny)))


def silu(x):
    half = 0.5 * x
    return half + half * jnp.tanh(half)


def shifted(x, col):
    if col == 1:
        return x
    lane = lax.broadcasted_iota(jnp.int32, x.shape, x.ndim - 1)
    if col == 0:
        return jnp.where(lane == 0, 0.0, pltpu.roll(x, 1, axis=x.ndim - 1))
    return jnp.where(lane == LANES - 1, 0.0, pltpu.roll(x, LANES - 1, axis=x.ndim - 1))


def kernel(
    nz, ny, nsteps, channels, temb, height,
    traj_h, noise_h, ts_h, w_in_h, w_one_h, w_two_h, w_out_h, wt1_h, wt2_h, wtp_h,
    out_ref,
    traj, noise, ts, w_in, w_one, w_two, w_out, wt1, wt2, wtp,
    win_f, win_m, wone_m, wtwo_m, wout_f,
    xbuf, xcol, h0, h1, rr, acts, vt, mcol, scol, tcol,
    msg, sums, terms, tbuf,
    load_sem, x_send, x_recv, h_send, h_recv, ar_send, ar_recv, t_send, t_recv, line_sem, end_sem,
):
    nrow = nz * ny
    row = lax.axis_index("row")
    step = lax.axis_index("step")
    mz, my = row // ny, lax.rem(row, ny)
    peers = [
        lax.rem(mz + dz, nz) * ny + lax.rem(my + dy, ny) for dz, dy in offsets(nz, ny)
    ]
    others = [lax.rem(step + d, nsteps) for d in range(1, nsteps)]
    below = lax.rem(row + 1, nrow)
    above = lax.rem(row + nrow - 1, nrow)
    per_group = channels // GROUPS

    terms[...] = jnp.zeros_like(terms)

    def at_end(y):
        return (y == 0) | (y == ny - 1) if ny >= 4 else y < 0

    column = [lax.rem(mz + d, nz) * ny + my for d in range(1, nz)]
    line = [mz * ny + lax.rem(my + d, ny) for d in range(1, ny)]
    barrier = pltpu.get_barrier_semaphore()
    for p in column + [above, below]:
        pl.semaphore_signal(barrier, inc=1, device_id={"row": p}, device_id_type=MESH)
    for d, p in enumerate(line, 1):
        @pl.when(jnp.logical_not(at_end(lax.rem(my + d, ny))))
        def _():
            pl.semaphore_signal(barrier, inc=1, device_id={"row": p}, device_id_type=MESH)
    for s in others:
        pl.semaphore_signal(barrier, inc=1, device_id={"step": s}, device_id_type=MESH)

    loads = [
        (traj_h, traj), (noise_h, noise), (ts_h, ts), (w_in_h, w_in), (w_one_h, w_one),
        (wt1_h, wt1), (wt2_h, wt2), (wtp_h, wtp), (w_two_h, w_two), (w_out_h, w_out),
    ]
    copies = [
        pltpu.make_async_copy(src, dst, load_sem.at[i]) for i, (src, dst) in enumerate(loads)
    ]
    for c in copies:
        c.start()
    (c_traj, c_noise, c_ts, c_win, c_wone, c_wt1, c_wt2, c_wtp, c_wtwo, c_wout) = copies

    c_traj.wait()
    for r in range(ROWS):
        xbuf[2 + r] = traj[0, :, r, :]

    xcol[...] = jnp.zeros_like(xcol)
    win_f[...] = jnp.zeros_like(win_f)
    c_win.wait()
    for p in range(3):
        for q in range(3):
            tap = 4 * (3 * p + q)
            win_f[tap : tap + 4, :channels] = w_in[p, q].astype(F32)
    win_m[...] = jnp.transpose(win_f[...])[:channels].astype(BF16)

    here = at_end(my)
    pl.semaphore_wait(barrier, nz - 1 + 2 + nsteps - 1 + jnp.where(here, 0, ny - 1))

    up = pltpu.make_async_remote_copy(
        xbuf.at[pl.ds(2, 2)], xbuf.at[pl.ds(6, 2)], x_send.at[0], x_recv.at[0],
        device_id={"row": above}, device_id_type=MESH,
    )
    down = pltpu.make_async_remote_copy(
        xbuf.at[pl.ds(4, 2)], xbuf.at[pl.ds(0, 2)], x_send.at[1], x_recv.at[1],
        device_id={"row": below}, device_id_type=MESH,
    )
    up.start()
    down.start()
    if ny >= 4:
        @pl.when((my == 1) | (my == ny - 2))
        def _():
            pl.semaphore_signal(
                end_sem, inc=1, device_id={"row": jnp.where(my == 1, above, below)},
                device_id_type=MESH,
            )

        @pl.when(here)
        def _():
            pl.semaphore_wait(end_sem, 1)

    for p in column:
        pl.semaphore_signal(line_sem, inc=1, device_id={"row": p}, device_id_type=MESH)

    def merge(weights, merged):
        for q in range(3):
            merged[q] = jnp.concatenate([weights[p, q] for p in range(3)], axis=1)

    c_wone.wait()
    merge(w_one, wone_m)

    is_top = row == 0
    is_bottom = row == nrow - 1

    def send_sums(k, line):
        msg[k] = line
        sums[k, pl.ds(row, 1), :] = line
        for p in peers:
            pltpu.make_async_remote_copy(
                msg.at[k], sums.at[k, pl.ds(row, 1), :], ar_send.at[k], ar_recv.at[k],
                device_id={"row": p}, device_id_type=MESH,
            ).start()

    def others_of(k):
        return sums.at[k, pl.ds(0, nrow - 1), :]

    def total_sums(k):
        part = others_of(k)
        pltpu.make_async_copy(part, part, ar_recv.at[k]).wait()
        return jnp.sum(sums[k], axis=0, keepdims=True)

    group_of = lax.broadcasted_iota(jnp.int32, (GROUPS, channels), 0) * per_group
    channel = lax.broadcasted_iota(jnp.int32, (GROUPS, channels), 1)
    members = jnp.where(
        (channel >= group_of) & (channel < group_of + per_group), 1.0, 0.0
    ).astype(BF16)

    def group_line(rows):
        total = functools.reduce(lambda a, b: a + b, rows)
        square = functools.reduce(lambda a, b: a + b, [v * v for v in rows])
        lane = lax.broadcasted_iota(jnp.int32, total.shape, 1)
        both = jnp.where(
            lane < LANES // 2,
            total + pltpu.roll(total, LANES // 2, axis=1),
            square + pltpu.roll(square, LANES // 2, axis=1),
        )
        high = both.astype(BF16)
        rest = both - high.astype(F32)
        mid = rest.astype(BF16)
        low = (rest - mid.astype(F32)).astype(BF16)
        grouped = dot(members, jnp.concatenate([high, mid, low], axis=1))
        grouped = grouped[:, :LANES] + grouped[:, LANES : 2 * LANES] + grouped[:, 2 * LANES :]
        stacked = jnp.concatenate(
            [grouped, pltpu.roll(grouped, LANES // 2, axis=1), jnp.zeros((64, LANES), F32)], axis=0
        )
        return jnp.sum(jnp.transpose(stacked)[: LANES // 2], axis=0, keepdims=True)

    count = per_group * height * LANES

    def norm_columns(k):
        total = total_sums(k) * (1.0 / count)
        columns = jnp.transpose(jnp.broadcast_to(total, (LANES, LANES)))
        mean, square = columns[:GROUPS], columns[GROUPS : 2 * GROUPS]
        vt[:GROUPS, :] = mean
        vt[GROUPS:, :] = 0.5 * lax.rsqrt(square - mean * mean + NORM_EPS)
        sub = lax.broadcasted_iota(jnp.int32, (8, LANES), 0)
        for first, target in ((0, mcol), (GROUPS, scol)):
            for j in range(channels // 8):
                low, high = 8 * j // per_group, (8 * j + 7) // per_group
                value = jnp.broadcast_to(vt[first + low : first + low + 1, :], (8, LANES))
                if high != low:
                    other = jnp.broadcast_to(vt[first + high : first + high + 1, :], (8, LANES))
                    value = jnp.where(sub < high * per_group - 8 * j, value, other)
                target[8 * j : 8 * j + 8, :] = value

    def activate(source, r):
        half = (source[r] - mcol[...]) * scol[...]
        act = half + half * jnp.tanh(half)
        if r == 0:
            act = jnp.where(is_top, 0.0, act)
        if r == ROWS + 1:
            act = jnp.where(is_bottom, 0.0, act)
        return act.astype(BF16)

    def place(r, act):
        for p in range(3):
            if 0 <= r - p < ROWS:
                acts[p * channels : (p + 1) * channels, (r - p) * LANES : (r - p + 1) * LANES] = act

    def conv(merged, source, finish):
        for half in range(ROWS // 2):
            for r in range(ROWS) if half == 0 else (ROWS, ROWS + 1):
                place(r, activate(source, r))
            x = acts[:, half * 2 * LANES : (half + 1) * 2 * LANES]
            y = [dot(merged[q], x) for q in range(3)]
            for i in range(2):
                cut = slice(i * LANES, (i + 1) * LANES)
                finish(2 * half + i, sum(shifted(y[q][:, cut], q) for q in range(3)))

    def halo_copies(buf, k):
        return [
            pltpu.make_async_remote_copy(
                buf.at[1], buf.at[ROWS + 1], h_send.at[k, 0], h_recv.at[k, 0],
                device_id={"row": above}, device_id_type=MESH,
            ),
            pltpu.make_async_remote_copy(
                buf.at[ROWS], buf.at[0], h_send.at[k, 1], h_recv.at[k, 1],
                device_id={"row": below}, device_id_type=MESH,
            ),
        ]

    up.wait_recv()
    down.wait_recv()
    for r in range(ROWS + 4):
        x = xbuf[r]
        if r < 2:
            x = jnp.where(is_top, 0.0, x)
        if r >= ROWS + 2:
            x = jnp.where(is_bottom, 0.0, x)
        for q in range(3):
            moved = shifted(x, q)
            for p in range(3):
                if 0 <= r - p < ROWS + 2:
                    tap = 4 * (3 * p + q)
                    xcol[tap : tap + 4, (r - p) * LANES : (r - p + 1) * LANES] = moved
    first = dot(win_m[:, :48], xcol[...].astype(BF16))
    for r in range(ROWS + 2):
        h0[r] = first[:, r * LANES : (r + 1) * LANES]
    first_line = group_line([h0[r] for r in range(1, ROWS + 1)])
    pl.semaphore_wait(line_sem, nz - 1)
    send_sums(0, first_line)

    c_ts.wait()
    times = ts[...].astype(F32)
    level = jnp.broadcast_to(times[:, 0:1], (1, LANES))
    level_next = jnp.broadcast_to(times[:, 1:2], (1, LANES))
    c_wt1.wait()
    half = channels // 2
    lane = lax.broadcasted_iota(jnp.int32, (LANES, channels), 1)
    place_of = jnp.where(lane < half, lane, lane - half).astype(F32)
    freq = jnp.exp(-math.log(10000.0) * place_of / half)
    angle = jnp.broadcast_to(times[:, 0:1], (LANES, channels)) * freq
    embed = jnp.where(lane < half, jnp.cos(angle), jnp.sin(angle)).astype(BF16)
    hidden = silu(dot(embed, wt1[...])).astype(BF16)
    c_wt2.wait()
    second = silu(dot(hidden, wt2[...])).astype(BF16)
    c_wtp.wait()
    tcol[...] = lax.dot_general(
        wtp[...], second, (((1,), (1,)), ((), ())), preferred_element_type=F32
    )

    c_wtwo.wait()
    merge(w_two, wtwo_m)
    c_wout.wait()
    wout_f[...] = jnp.zeros_like(wout_f)
    for p in range(3):
        for q in range(3):
            tap = 8 * (3 * p + q)
            wout_f[tap : tap + 4, :] = w_out[p, q].astype(F32)

    def alpha_bar(t):
        return jnp.cos((t / 1000.0 + 0.008) / 1.008 * (math.pi / 2)) ** 2

    now, after = alpha_bar(level), alpha_bar(level_next)
    sigma = NOISE_SHARE * jnp.sqrt((1.0 - after) / (1.0 - now) * (1.0 - now / after))
    keep_x = jnp.sqrt(after / now)
    keep_e = jnp.sqrt(1.0 - after - sigma * sigma) - jnp.sqrt(after) * jnp.sqrt(
        1.0 - now
    ) / jnp.sqrt(now)

    norm_columns(0)

    def finish_one(r, value):
        h1[1 + r] = value + tcol[...]

    conv(wone_m, h0, finish_one)
    halo1 = halo_copies(h1, 0)
    send_sums(1, group_line([h1[r] for r in range(1, ROWS + 1)]))
    for c in halo1:
        c.start()

    norm_columns(1)
    for c in halo1:
        c.wait_recv()

    def finish_two(r, value):
        rr[1 + r] = value + h0[1 + r]

    conv(wtwo_m, h1, finish_two)
    halo2 = halo_copies(rr, 1)
    send_sums(2, group_line([rr[r] for r in range(1, ROWS + 1)]))
    for c in halo2:
        c.start()

    c_noise.wait()
    norm_columns(2)
    for c in halo2:
        c.wait_recv()
    a3 = jnp.concatenate([activate(rr, r) for r in range(ROWS + 2)], axis=1)
    y = dot(wout_f[...].astype(BF16), a3)
    is_first = step == 0
    for r in range(ROWS):
        eps = jnp.zeros((8, LANES), F32)
        for q in range(3):
            column = jnp.zeros((8, LANES), F32)
            for p in range(3):
                tap = 8 * (3 * p + q)
                column += y[tap : tap + 8, (r + p) * LANES : (r + p + 1) * LANES]
            eps += shifted(column, q)
        x = traj[0, :, r, :]
        term = keep_x * x + keep_e * eps[:LATENT] + sigma * noise[0, :, r, :] - x
        term = term + jnp.where(is_first, x, 0.0)
        tbuf[r] = term

    def to_later(d):
        return pltpu.make_async_remote_copy(
            tbuf, terms.at[step], t_send.at[d - 1], t_recv.at[step],
            device_id={"step": lax.rem(step + d, nsteps)}, device_id_type=MESH,
        )

    for d in range(nsteps - 1, 0, -1):
        @pl.when(step + d < nsteps)
        def _():
            to_later(d).start()
    for s in range(nsteps - 1):
        @pl.when(s < step)
        def _():
            pltpu.make_async_copy(tbuf, tbuf, t_recv.at[s]).wait()
    error = jnp.zeros((LATENT, LANES), F32)
    for r in range(ROWS):
        earlier = jnp.zeros((LATENT, LANES), F32)
        for s in range(nsteps - 1):
            earlier = earlier + terms[s, r]
        out_ref[0, :LATENT, r, :] = earlier + tbuf[r]
        x = traj[0, :, r, :]
        gap = jnp.where(is_first, 0.0, earlier - x)
        error = error + gap * gap
    send_sums(3, jnp.sum(error, axis=0, keepdims=True))
    up.wait_send()
    down.wait_send()
    for c in halo1 + halo2:
        c.wait_send()
    for k in range(3):
        part = others_of(k)
        pltpu.make_async_copy(part, part, ar_send.at[k]).wait()
    for d in range(1, nsteps):
        @pl.when(step + d < nsteps)
        def _():
            to_later(d).wait_send()

    whole = jnp.sum(total_sums(3), axis=1, keepdims=True)
    out_ref[0, LATENT] = jnp.broadcast_to(
        whole * (1.0 / (LATENT * height * LANES)), (ROWS, LANES)
    )

    part = others_of(3)
    pltpu.make_async_copy(part, part, ar_send.at[3]).wait()


def finish(both, advanced_out, error_out, error, sem):
    copies = [
        pltpu.make_async_copy(both.at[:, pl.ds(0, LATENT)], advanced_out, sem.at[0]),
        pltpu.make_async_copy(error, error_out, sem.at[1]),
    ]
    copies[0].start()
    error[...] = both[0, LATENT, 0:1, 0:1]
    copies[1].start()
    for c in copies:
        c.wait()


def shards(nz, ny, nsteps, trajectory, noise, tsteps, w_in, w_one, w_two, w_out, wt1, wt2, wtp):
    w_in = jnp.transpose(w_in, (0, 1, 3, 2))
    wtp = jnp.transpose(wtp)
    args = (trajectory, noise, tsteps, w_in, w_one, w_two, w_out, wt1, wt2, wtp)
    channels, temb = wt1.shape
    nrow = nz * ny
    height = trajectory.shape[2] * nrow
    vmem = lambda shape, dtype: pltpu.VMEM(shape, dtype)
    scratch = [vmem(a.shape, a.dtype) for a in args] + [
        vmem((LANES, -(-channels // LANES) * LANES), F32),
        vmem((channels, LANES), BF16),
        vmem((3, channels, 3 * channels), BF16),
        vmem((3, channels, 3 * channels), BF16),
        vmem((80, channels), F32),
        vmem((ROWS + 4, LATENT, LANES), F32),
        vmem((48, (ROWS + 2) * LANES), F32),
        vmem((ROWS + 2, channels, LANES), F32),
        vmem((ROWS + 2, channels, LANES), F32),
        vmem((ROWS + 2, channels, LANES), F32),
        vmem((3 * channels, ROWS * LANES), BF16),
        vmem((2 * GROUPS, LANES), F32),
        vmem((channels, LANES), F32),
        vmem((channels, LANES), F32),
        vmem((channels, LANES), F32),
        vmem((4, 1, LANES), F32),
        vmem((4, nrow, LANES), F32),
        vmem((nsteps - 1, ROWS, LATENT, LANES), F32),
        vmem((ROWS, LATENT, LANES), F32),
        pltpu.SemaphoreType.DMA((len(args),)),
        pltpu.SemaphoreType.DMA((2,)),
        pltpu.SemaphoreType.DMA((2,)),
        pltpu.SemaphoreType.DMA((2, 2)),
        pltpu.SemaphoreType.DMA((2, 2)),
        pltpu.SemaphoreType.DMA((4,)),
        pltpu.SemaphoreType.DMA((4,)),
        pltpu.SemaphoreType.DMA((nsteps - 1,)),
        pltpu.SemaphoreType.DMA((nsteps - 1,)),
        pltpu.SemaphoreType.REGULAR,
        pltpu.SemaphoreType.REGULAR,
    ]
    both = pl.pallas_call(
        functools.partial(kernel, nz, ny, nsteps, channels, temb, height),
        out_shape=pltpu.VMEM((1, LATENT + 1, ROWS, LANES), F32),
        in_specs=[pl.BlockSpec(memory_space=pltpu.HBM)] * len(args),
        out_specs=pl.BlockSpec(memory_space=pltpu.VMEM),
        scratch_shapes=scratch,
        compiler_params=pltpu.CompilerParams(
            collective_id=0, has_side_effects=True, vmem_limit_bytes=56 * 1024 * 1024
        ),
    )(*args)
    advanced, error = pl.pallas_call(
        finish,
        out_shape=(
            jax.ShapeDtypeStruct(trajectory.shape, F32),
            jax.ShapeDtypeStruct((1, 1), F32),
        ),
        in_specs=[pl.BlockSpec(memory_space=pltpu.VMEM)],
        out_specs=(pl.BlockSpec(memory_space=pltpu.HBM),) * 2,
        scratch_shapes=[pltpu.VMEM((1, 1), F32), pltpu.SemaphoreType.DMA((2,))],
    )(pltpu.with_memory_space_constraint(both, pltpu.VMEM))
    return advanced, error.reshape(1)


def solution(mesh):
    nsteps, nrow = mesh.shape["step"], mesh.shape["row"]
    ny = 8 if nrow % 64 == 0 else max(1, nrow // 2)
    place = P("step", None, "row", None)
    return jax.shard_map(
        functools.partial(shards, nrow // ny, ny, nsteps),
        mesh=mesh,
        in_specs=(place, place, P("step", None)) + (P(),) * 7,
        out_specs=(place, P("step")),
        check_vma=False,
    )
```
